512 devices in a mesh: dp: 32 (over y, x_lo, core), panel: 16 (over z, x_hi).
Axes of the slice: x: 4 (x_hi: 2, x_lo: 2; x = x_hi * 2 + x_lo), y: 8, z: 8, core: 2. Of those that a mesh axis runs over, the one named last changes fastest.
Arguments:
- out_grads: bfloat16 [6144, 8256], P('dp', 'panel'), may hold values from -6 to 6
- layer_inputs: bfloat16 [6144, 2048], P('dp'), may hold values from -0.4375 to 0.4375
- query_grads: bfloat16 [512, 8256], P('dp', 'panel'), may hold values from -6 to 6
- query_inputs: bfloat16 [512, 2048], P('dp'), may hold values from -0.25 to 0.25
- basis_out: bfloat16 [8256, 8256], P('panel', 'dp'), may hold values from -0.125 to 0.125
- basis_in: bfloat16 [2048, 2048], P(None, 'panel'), may hold values from -0.125 to 0.125
Outputs:
- eigen_values: float32 [8256, 2048], P('dp', 'panel')
- preconditioned: bfloat16 [8256, 2048], P('dp', 'panel')
The draws below stay inside these ranges and needn't reach their ends.
All inputs are finite; a program needn't handle non-finite values.
Results may differ from the reference program's by a relative error of at most 0.033.
Values may be sent and summed in bfloat16 or wider, within the bound.
A program may use at most 64 MiB of HBM per device.

```python
import jax
import jax.numpy as jnp
from jax import lax

FW = 8256
DW = 2048
SEQ_LEN = 192
TOKENS = 6144
QLEN = 512
N_DP = 32
N_PANEL = 16


def raised(drawn, rng, source, target, blocks, factor):
    owner, partner = [(jnp.arange(drawn.shape[position]) // (drawn.shape[position] // blocks)).reshape([-1 if axis == position else 1 for axis in range(drawn.ndim)]) for position in (source, target)]
    chosen = jax.random.permutation(rng, blocks)[partner]
    strong = (owner == chosen) | (owner == (partner + blocks // 2) % blocks)
    return jnp.where(strong, factor * drawn, drawn)


def levels(own_key, extent, shards, smallest, high):
    def one(position, parts):
        draws = jax.random.uniform(jax.random.fold_in(jax.random.fold_in(own_key, 6), position), (parts,), jnp.float32, smallest / len(shards), high / len(shards))
        return jnp.repeat(jnp.exp(draws), extent[position] // parts).reshape((-1,) + (1,) * (len(extent) - position - 1))

    level = one(*shards[0])
    for cut in shards[1:]:
        level = level * one(*cut)
    return level


def noise(own_key, extent, scale, limit, cuts=(), kind=jnp.bfloat16):
    level = levels(own_key, extent, cuts, -0.22, 0.18) if cuts else 1.0
    values = jax.random.normal(own_key, extent, jnp.float32) * scale * level
    return jnp.minimum(jnp.maximum(values, -limit), limit).astype(kind)


def heavy_noise(own_key, extent, deviation, limit, shards, heavy, dtype=jnp.bfloat16):
    drawn = deviation * jax.random.normal(own_key, extent, jnp.float32)
    if shards:
        drawn = drawn * levels(own_key, extent, shards, -0.22, 0.18)
    return jnp.clip(raised(drawn, jax.random.fold_in(own_key, 3), *heavy), -limit, limit).astype(dtype)


def setup_inputs(seed: int = 0) -> dict:
    key_list = jax.random.split(jax.random.key(seed), 7)
    out_grads = noise(key_list[0], (TOKENS, FW), 1.0, 6.0, ((0, 32), (1, 16)))
    layer_inputs = noise(key_list[1], (TOKENS, DW), SEQ_LEN ** -0.5, 0.4375, ((0, 32),))
    query_grads = noise(key_list[2], (QLEN, FW), 1.0, 6.0, ((0, 32), (1, 16)))
    query_inputs = noise(key_list[3], (QLEN, DW), QLEN ** -0.5, 0.25, ((0, 32),))
    basis_out = heavy_noise(key_list[4], (FW, FW), FW ** -0.5, 0.125, ((0, 16), (1, 32)), (1, 0, 32, 2.75))
    basis_in = noise(key_list[5], (DW, DW), DW ** -0.5, 0.125, ((1, 16),))
    return dict(out_grads=out_grads, layer_inputs=layer_inputs, query_grads=query_grads, query_inputs=query_inputs, basis_out=basis_out, basis_in=basis_in)


damping = 0.1


def rounded(values):
    return lax.optimization_barrier(values.astype(jnp.bfloat16)).astype(jnp.float32)


def rotate_rows(grads, basis_out):
    width = FW // N_PANEL
    total = jnp.zeros((grads.shape[0], FW), jnp.float32)
    for block in range(N_PANEL):
        low = block * width
        part = jnp.dot(grads[:, low:low + width], basis_out[low:low + width, :], preferred_element_type=jnp.float32)
        total = total + rounded(part)
    return total.astype(jnp.bfloat16)


def reference(out_grads, layer_inputs, query_grads, query_inputs, basis_out, basis_in):
    fit_rot = rotate_rows(out_grads, basis_out)
    query_rot = rotate_rows(query_grads, basis_out)
    fit_in = jnp.dot(layer_inputs, basis_in, preferred_element_type=jnp.float32).astype(jnp.bfloat16)
    query_in = jnp.dot(query_inputs, basis_in, preferred_element_type=jnp.float32).astype(jnp.bfloat16)

    def add_sequence(carry, pair):
        grad_part, input_part = pair
        rotated = jnp.dot(grad_part.T, input_part, preferred_element_type=jnp.float32)
        return carry + rotated * rotated, None

    squares, unused = lax.scan(add_sequence, jnp.zeros((FW, DW), jnp.float32),
                               (fit_rot.reshape(N_DP, SEQ_LEN, FW), fit_in.reshape(N_DP, SEQ_LEN, DW)))
    eigen_values = squares / N_DP
    query_sum = jnp.dot(query_rot.T, query_in, preferred_element_type=jnp.float32)
    scaled = (query_sum / (eigen_values + damping)).astype(jnp.bfloat16)
    width_in = DW // N_PANEL
    image_sum = jnp.zeros((DW, FW), jnp.float32)
    for block in range(N_PANEL):
        low = block * width_in
        part = jnp.dot(basis_in[:, low:low + width_in], scaled[:, low:low + width_in].T, preferred_element_type=jnp.float32)
        image_sum = image_sum + rounded(part)
    image = image_sum.astype(jnp.bfloat16)
    width_out = FW // N_DP
    result = jnp.zeros((FW, DW), jnp.float32)
    for block in range(N_DP):
        low = block * width_out
        part = jnp.dot(basis_out[:, low:low + width_out], image[:, low:low + width_out].T, preferred_element_type=jnp.float32)
        result = result + rounded(part)
    return eigen_values, result.astype(jnp.bfloat16)
```

```python
import functools

import jax
import jax.numpy as jnp
from jax import lax
from jax.experimental import pallas as pl
from jax.experimental.pallas import tpu as pltpu
from jax.sharding import PartitionSpec as P

damping = 0.1
bf16 = jnp.bfloat16
f32 = jnp.float32
SEQ = 192
TOK = 208
COL = 258
PAD = 272
MAIN = 512
N_SEQ = 32
RING = 8
NT = (((1,), (1,)), ((), ()))


def coords():
    dp, panel = lax.axis_index("dp"), lax.axis_index("panel")
    y, xl, c = lax.div(dp, 4), lax.rem(lax.div(dp, 2), 2), lax.rem(dp, 2)
    return y, xl, c, lax.div(panel, 2), lax.rem(panel, 2)


def device(y, xl, c, z, xh):
    return (y * 4 + xl * 2 + c, z * 2 + xh)


def turn(pos, by):
    return lax.rem(pos + by + RING, RING)


def x_device(x, y, c, z):
    x = lax.rem(x + 4, 4)
    return device(y, lax.rem(x, 2), c, z, lax.div(x, 2))


def signal(who):
    pl.semaphore_signal(
        pltpu.get_barrier_semaphore(), inc=1, device_id=who, device_id_type=pl.DeviceIdType.MESH
    )


def wait_all(count):
    pl.semaphore_wait(pltpu.get_barrier_semaphore(), count)


class Copies:
    def __init__(self, send, recv):
        self.send, self.recv, self.used, self.started = send, recv, 0, []

    def make(self, src, dst, who):
        k = self.used
        self.used += 1
        return pltpu.make_async_remote_copy(
            src_ref=src, dst_ref=dst, send_sem=self.send.at[k], recv_sem=self.recv.at[k],
            device_id=who, device_id_type=pl.DeviceIdType.MESH,
        )

    def start(self, src, dst, who):
        copy = self.make(src, dst, who)
        copy.start()
        self.started.append(copy)
        return copy

    def finish(self):
        for copy in self.started:
            copy.wait_send()


def permute(copies, local_sem, src, dst, who, same):
    copy = copies.make(src, dst, who)
    local = pltpu.make_async_copy(src, dst, local_sem)

    @pl.when(jnp.logical_not(same))
    def _():
        copy.start()

    @pl.when(same)
    def _():
        local.start()

    def wait():
        @pl.when(jnp.logical_not(same))
        def _():
            copy.wait()

        @pl.when(same)
        def _():
            local.wait()

    return wait


def gather_ring(copies, pos, up, down, slot, ready=None):
    ups = copies.start(slot(pos), slot(pos), up)
    downs = copies.start(slot(pos), slot(pos), down)
    if ready is not None:
        ready(pos)
    for t in range(1, 5):
        at = turn(pos, -t)
        ups.wait_recv()
        if t < 4:
            ups = copies.start(slot(at), slot(at), up)
        if ready is not None:
            ready(at)
        if t < 4:
            at = turn(pos, t)
            downs.wait_recv()
            if t < 3:
                downs = copies.start(slot(at), slot(at), down)
            if ready is not None:
                ready(at)


def scatter_ring(copies, pos, up, down, chunk, sent, got):
    ups = downs = None
    for t in range(4):
        value = chunk(turn(pos, 4 - t))
        if t:
            ups.wait_recv()
        for a, part in enumerate(value):
            total = part + got[t - 1, a].astype(f32) if t else part
            sent[t, a] = total.astype(bf16)
        ups = copies.start(sent.at[t], got.at[t], up)
        if t < 3:
            value = chunk(turn(pos, t - 3))
            if t:
                downs.wait_recv()
            for a, part in enumerate(value):
                total = part + got[3 + t, a].astype(f32) if t else part
                sent[4 + t, a] = total.astype(bf16)
            downs = copies.start(sent.at[4 + t], got.at[4 + t], down)
    value = chunk(pos)
    ups.wait_recv()
    downs.wait_recv()
    return [
        part + got[3, a].astype(f32) + got[6, a].astype(f32) for a, part in enumerate(value)
    ]


def gather_kernel(gm, gt, f, bm, bt, gm_out, gt_out, f_out, bm_out, bt_out, send, recv, local):
    y, xl, c, z, xh = coords()
    x = xh * 2 + xl
    other = device(y, xl, 1 - c, z, xh)
    up, down = device(turn(y, 1), xl, c, z, xh), device(turn(y, -1), xl, c, z, xh)
    right, left = x_device(x + 1, y, c, z), x_device(x + 3, y, c, z)
    pair = device(y, 1 - xl, c, z, xh)
    g_to, g_from = device(y, c, xh, z, xl), device(y, xh, xl, z, c)
    g_same = jnp.logical_and(xh == xl, xl == c)
    f_to = device(z, xh, c, y, xl)
    f_same = jnp.logical_and(y == z, xl == xh)

    for who in (other, up, down, right, left):
        signal(who)

    @pl.when(jnp.logical_not(g_same))
    def _():
        signal(g_from)

    @pl.when(jnp.logical_not(f_same))
    def _():
        signal(f_to)

    wait_all(7 - g_same.astype(jnp.int32) - f_same.astype(jnp.int32))

    copies = Copies(send, recv)
    g_wait = permute(copies, local.at[0], gm, gm_out.at[xh, y], g_to, g_same)
    t_wait = permute(copies, local.at[1], gt, gt_out.at[y, xh], g_to, g_same)
    f_wait = permute(copies, local.at[2], f, f_out.at[c, z, xh], f_to, f_same)

    own_m = pltpu.make_async_copy(bm, bm_out.at[x], local.at[3])
    own_t = pltpu.make_async_copy(bt, bt_out.at[x], local.at[4])
    own_m.start()
    own_t.start()
    m_right = copies.start(bm, bm_out.at[x], right)
    m_left = copies.start(bm, bm_out.at[x], left)
    t_right = copies.start(bt, bt_out.at[x], right)
    t_left = copies.start(bt, bt_out.at[x], left)

    g_wait()
    t_wait()
    forwards = []

    def pass_on(ref):
        def ready(at):
            forwards.append(copies.start(ref(at), ref(at), other))

        return ready

    def slots_g(at):
        return gm_out.at[c, at]

    def slots_t(at):
        return gt_out.at[at, c]

    def slots_f(at):
        return f_out.at[c, at]

    f_wait()
    swapped = copies.start(f_out.at[c, y, xl], f_out.at[c, y, xl], pair)
    gather_ring(copies, y, up, down, slots_g, pass_on(slots_g))
    x_l, x_r = lax.rem(x + 3, 4), lax.rem(x + 1, 4)
    m_right.wait_recv()
    far_a = copies.start(
        bm_out.at[x_l, pl.ds(0, 144)], bm_out.at[x_l, pl.ds(0, 144)], right
    )
    m_left.wait_recv()
    far_b = copies.start(
        bm_out.at[x_r, pl.ds(144, 128)], bm_out.at[x_r, pl.ds(144, 128)], left
    )
    t_right.wait_recv()
    t_left.wait_recv()
    far_t = copies.start(bt_out.at[x_l], bt_out.at[x_l], right)
    gather_ring(copies, y, up, down, slots_t, pass_on(slots_t))
    swapped.wait_recv()
    gather_ring(copies, y, up, down, slots_f, pass_on(slots_f))
    far_a.wait_recv()
    far_b.wait_recv()
    far_t.wait_recv()
    for copy in forwards:
        copy.wait_recv()
    own_m.wait()
    own_t.wait()
    copies.finish()


def rotate_kernel(bm, bt, gm, gt, out, sent, got, stage, landed, send, recv):
    y, xl, c, z, xh = coords()
    up, down = device(y, xl, c, turn(z, 1), xh), device(y, xl, c, turn(z, -1), xh)
    pair = device(y, 1 - xl, c, z, xh)
    for who in (up, down, pair):
        signal(who)
    wait_all(3)
    copies = Copies(send, recv)

    def chunk(d):
        part = lax.dot_general(bm[0], gm[0, d], NT, preferred_element_type=f32)
        part += lax.dot_general(bm[1], gm[1, d], NT, preferred_element_type=f32)
        part += jnp.dot(bt[...], gt[d], preferred_element_type=f32)[:, :TOK]
        return [part]

    (total,) = scatter_ring(copies, z, up, down, chunk, sent, got)
    stage[0] = total[:PAD].astype(bf16)
    stage[1] = total[PAD:].astype(bf16)
    swap = copies.start(stage.at[1 - xl], landed, pair)
    out[xl] = stage[xl]
    swap.wait_recv()
    out[1 - xl] = landed[...]
    copies.finish()


def solve_kernel(
    rot, f, bo, bi, eig, pre,
    lhs, sent_a, got_a, tot_a, stage_a, land_a, s_buf, core_s, core_r,
    sent_b, got_b, tot_b, stage_b, land_b, u_out, u_in,
    sent_c, got_c, tot_c, stage_c, land_c, send, recv, local,
):
    y, xl, c, z, xh = coords()
    other = device(y, xl, 1 - c, z, xh)
    y_up, y_down = device(turn(y, 1), xl, c, z, xh), device(turn(y, -1), xl, c, z, xh)
    z_up, z_down = device(y, xl, c, turn(z, 1), xh), device(y, xl, c, turn(z, -1), xh)
    pair_l, pair_h = device(y, 1 - xl, c, z, xh), device(y, xl, c, z, 1 - xh)
    u_to = device(z, xh, c, y, xl)
    u_same = jnp.logical_and(y == z, xl == xh)
    for who in (other, y_up, y_down, z_up, z_down, pair_l, pair_h):
        signal(who)

    @pl.when(jnp.logical_not(u_same))
    def _():
        signal(u_to)

    wait_all(8 - u_same.astype(jnp.int32))
    copies = Copies(send, recv)

    lane = lax.broadcasted_iota(jnp.int32, (PAD, TOK), 1)
    for h in range(2):
        value = rot[h]
        zero = jnp.zeros_like(value)
        lhs[h, :PAD] = jnp.where(lane < SEQ, value, zero)
        lhs[h, PAD:] = jnp.where(lane < SEQ, zero, value)

    def chunk_a(d):
        parts = []
        for side in range(2):
            first = jnp.dot(lhs[0], f[0, d, side], preferred_element_type=f32)
            second = jnp.dot(lhs[1], f[1, d, side], preferred_element_type=f32)
            parts.append(first[:PAD] * first[:PAD] + second[:PAD] * second[:PAD])
            parts.append(first[PAD:] + second[PAD:])
        return parts

    total = scatter_ring(copies, z, z_up, z_down, chunk_a, sent_a, got_a)
    for a, part in enumerate(total):
        tot_a[a // 2, a % 2] = part
    stage_a[...] = tot_a[1 - xh].astype(bf16)
    swap = copies.start(stage_a, land_a, pair_h)
    swap.wait_recv()
    values = (tot_a[xh, 0] + land_a[0].astype(f32)) / N_SEQ
    sums = tot_a[xh, 1] + land_a[1].astype(f32)
    eig[...] = values[:COL]
    s_buf[z, xh] = (sums / (values + damping)).astype(bf16)

    swap = copies.start(s_buf.at[z, xh], s_buf.at[z, xh], pair_h)
    swap.wait_recv()

    across = []

    def to_core(d):
        for side in range(2):
            core_s[d, side] = jnp.dot(
                bo[1 - c], s_buf[d, side], preferred_element_type=f32
            ).astype(bf16)

    gather_ring(copies, z, z_up, z_down, lambda at: s_buf.at[at])
    order = [turn(y, by) for by in (4, -3, 3, -2, 2, -1, 1, 0)]
    for d in order:
        to_core(d)
        across.append(copies.start(core_s.at[d], core_r.at[d], other))
    waits = iter(across)

    def chunk_b(d):
        parts = [
            jnp.dot(bo[c], s_buf[d, side], preferred_element_type=f32) for side in range(2)
        ]
        next(waits).wait_recv()
        return [part + core_r[d, side].astype(f32) for side, part in enumerate(parts)]

    total = scatter_ring(copies, y, y_up, y_down, chunk_b, sent_b, got_b)
    for a, part in enumerate(total):
        tot_b[a] = part
    stage_b[...] = tot_b[1 - xl].astype(bf16)
    swap = copies.start(stage_b, land_b, pair_l)
    swap.wait_recv()
    u_out[...] = (tot_b[xl] + land_b[...].astype(f32)).astype(bf16)
    permute(copies, local, u_out, u_in, u_to, u_same)()

    def chunk_c(d):
        return [
            lax.dot_general(u_in[...], bi[2 * d + side], NT, preferred_element_type=f32)
            for side in range(2)
        ]

    total = scatter_ring(copies, z, z_up, z_down, chunk_c, sent_c, got_c)
    for a, part in enumerate(total):
        tot_c[a] = part
    stage_c[...] = tot_c[1 - xh].astype(bf16)
    swap = copies.start(stage_c, land_c, pair_h)
    swap.wait_recv()
    pre[...] = (tot_c[xh] + land_c[...].astype(f32))[:COL].astype(bf16)
    copies.finish()


def params(number):
    return pltpu.CompilerParams(
        collective_id=number, has_side_effects=True, vmem_limit_bytes=48 * 2**20
    )


def per_device(out_grads, layer_inputs, query_grads, query_inputs, basis_out, basis_in):
    shape = jax.ShapeDtypeStruct
    anywhere, vmem = pl.BlockSpec(memory_space=pl.ANY), pl.BlockSpec(memory_space=pltpu.VMEM)
    dma = pltpu.SemaphoreType.DMA

    tokens = jnp.concatenate([out_grads, query_grads], axis=0)
    gm = tokens[:, :MAIN]
    gt = jnp.pad(tokens[:, MAIN:].T, ((0, 12), (0, 48)))
    f = jnp.concatenate(
        [
            jnp.dot(layer_inputs, basis_in, preferred_element_type=f32).astype(bf16),
            jnp.dot(query_inputs, basis_in, preferred_element_type=f32).astype(bf16),
        ],
        axis=0,
    )
    bm = jnp.pad(basis_out[:MAIN].T, ((0, PAD - COL), (0, 0)))
    bt = jnp.pad(basis_out[MAIN:], ((0, 12), (0, PAD - COL)))
    gm_all, gt_all, f_all, bm_all, bt_all = pl.pallas_call(
        gather_kernel,
        out_shape=[
            shape((2, RING, TOK, MAIN), bf16),
            shape((RING, 2, 16, 256), bf16),
            shape((2, RING, 2, TOK, 128), bf16),
            shape((4, PAD, MAIN), bf16),
            shape((4, 16, PAD), bf16),
        ],
        in_specs=[anywhere] * 5,
        out_specs=[anywhere] * 5,
        scratch_shapes=[dma((56,)), dma((56,)), dma((5,))],
        compiler_params=params(0),
    )(gm, gt, f, bm, bt)

    tail = bt_all.reshape(2, 2, 16, PAD).transpose(1, 3, 0, 2).reshape(2 * PAD, 32)
    rot = pl.pallas_call(
        rotate_kernel,
        out_shape=shape((2, PAD, TOK), bf16),
        in_specs=[vmem] * 4,
        out_specs=vmem,
        scratch_shapes=[
            pltpu.VMEM((7, 1, 2 * PAD, TOK), bf16),
            pltpu.VMEM((7, 1, 2 * PAD, TOK), bf16),
            pltpu.VMEM((2, PAD, TOK), bf16),
            pltpu.VMEM((PAD, TOK), bf16),
            dma((8,)),
            dma((8,)),
        ],
        compiler_params=params(1),
    )(bm_all.reshape(2, 2 * PAD, MAIN), tail, gm_all, gt_all.reshape(RING, 32, 256))

    bo = jnp.pad(
        basis_out.reshape(2, COL, COL), ((0, 0), (0, PAD - COL), (0, PAD - COL))
    )

    def buffers(parts):
        return [
            pltpu.VMEM((7, parts, PAD, 128), bf16),
            pltpu.VMEM((7, parts, PAD, 128), bf16),
        ]

    return pl.pallas_call(
        solve_kernel,
        out_shape=[shape((COL, 128), f32), shape((COL, 128), bf16)],
        in_specs=[vmem] * 4,
        out_specs=[vmem] * 2,
        scratch_shapes=[
            pltpu.VMEM((2, 2 * PAD, TOK), bf16),
            *buffers(4),
            pltpu.VMEM((2, 2, PAD, 128), f32),
            pltpu.VMEM((2, PAD, 128), bf16),
            pltpu.VMEM((2, PAD, 128), bf16),
            pltpu.VMEM((RING, 2, PAD, 128), bf16),
            pltpu.VMEM((RING, 2, PAD, 128), bf16),
            pltpu.VMEM((RING, 2, PAD, 128), bf16),
            *buffers(2),
            pltpu.VMEM((2, PAD, 128), f32),
            pltpu.VMEM((PAD, 128), bf16),
            pltpu.VMEM((PAD, 128), bf16),
            pltpu.VMEM((PAD, 128), bf16),
            pltpu.VMEM((PAD, 128), bf16),
            *buffers(2),
            pltpu.VMEM((2, PAD, 128), f32),
            pltpu.VMEM((PAD, 128), bf16),
            pltpu.VMEM((PAD, 128), bf16),
            dma((48,)),
            dma((48,)),
            dma,
        ],
        compiler_params=params(2),
    )(rot, f_all, bo, basis_in.reshape(16, 128, 128))


def solution(mesh):
    in_specs = (
        P("dp", "panel"),
        P("dp", None),
        P("dp", "panel"),
        P("dp", None),
        P("panel", "dp"),
        P(None, "panel"),
    )
    out_specs = (P("dp", "panel"), P("dp", "panel"))
    return jax.shard_map(
        per_device, mesh=mesh, in_specs=in_specs, out_specs=out_specs, check_vma=False
    )
```

```python
import jax
import jax.numpy as jnp
from jax import lax
from jax.experimental import pallas as pl
from jax.experimental.pallas import tpu as pltpu
from jax.sharding import PartitionSpec as P

damping = 0.1
bf16 = jnp.bfloat16
f32 = jnp.float32
SEQ = 192
TOK = 208
COL = 258
PAD = 272
MAIN = 512
N_SEQ = 32
RING = 8
NT = (((1,), (1,)), ((), ()))
TN = (((0,), (0,)), ((), ()))
N_SEM = 256


def coords():
    dp, panel = lax.axis_index("dp"), lax.axis_index("panel")
    y, xl, c = lax.div(dp, 4), lax.rem(lax.div(dp, 2), 2), lax.rem(dp, 2)
    return y, xl, c, lax.div(panel, 2), lax.rem(panel, 2)


def device(y, xl, c, z, xh):
    return (y * 4 + xl * 2 + c, z * 2 + xh)


def turn(pos, by):
    return lax.rem(pos + by + RING, RING)


def x_device(x, y, c, z):
    x = lax.rem(x + 4, 4)
    return device(y, lax.rem(x, 2), c, z, lax.div(x, 2))


def signal(who):
    pl.semaphore_signal(
        pltpu.get_barrier_semaphore(), inc=1, device_id=who, device_id_type=pl.DeviceIdType.MESH
    )


def wait_all(count):
    pl.semaphore_wait(pltpu.get_barrier_semaphore(), count)


class Copies:
    def __init__(self, send, recv):
        self.send, self.recv, self.used, self.started = send, recv, 0, []

    def make(self, src, dst, who):
        k = self.used
        self.used += 1
        return pltpu.make_async_remote_copy(
            src_ref=src, dst_ref=dst, send_sem=self.send.at[k], recv_sem=self.recv.at[k],
            device_id=who, device_id_type=pl.DeviceIdType.MESH,
        )

    def start(self, src, dst, who):
        copy = self.make(src, dst, who)
        copy.start()
        self.started.append(copy)
        return copy

    def finish(self):
        for copy in self.started:
            copy.wait_send()


def permute(copies, local_sem, src, dst, who, same):
    copy = copies.make(src, dst, who)
    local = pltpu.make_async_copy(src, dst, local_sem)

    @pl.when(jnp.logical_not(same))
    def _():
        copy.start()

    @pl.when(same)
    def _():
        local.start()

    def wait():
        @pl.when(jnp.logical_not(same))
        def _():
            copy.wait()

        @pl.when(same)
        def _():
            local.wait()

    return wait


def run(*streams):
    live = list(streams)
    while live:
        for stream in list(live):
            try:
                next(stream)
            except StopIteration:
                live.remove(stream)


def gather_stream(copies, pos, ways, sign, slot, ready=None, first=None):
    ahead, back = ways[::sign]
    if first is not None:
        yield
        first()
    a = copies.start(slot(pos), slot(pos), ahead)
    b = copies.start(slot(pos), slot(pos), back)
    if ready is not None:
        ready(pos)
    for t in range(1, 5):
        yield
        at = turn(pos, -sign * t)
        a.wait_recv()
        if t < 4:
            a = copies.start(slot(at), slot(at), ahead)
        if ready is not None:
            ready(at)
        if t < 4:
            yield
            at = turn(pos, sign * t)
            b.wait_recv()
            if t < 3:
                b = copies.start(slot(at), slot(at), back)
            if ready is not None:
                ready(at)


def scatter_stream(copies, pos, ways, sign, chunk, sent, got, done):
    ahead, back = ways[::sign]
    a = b = None
    for t in range(4):
        value = chunk(turn(pos, sign * (4 - t)))
        if t:
            yield
            a.wait_recv()
            value = value + got[t - 1].astype(f32)
        sent[t] = value.astype(bf16)
        a = copies.start(sent.at[t], got.at[t], ahead)
        if t < 3:
            value = chunk(turn(pos, sign * (t - 3)))
            if t:
                yield
                b.wait_recv()
                value = value + got[3 + t].astype(f32)
            sent[4 + t] = value.astype(bf16)
            b = copies.start(sent.at[4 + t], got.at[4 + t], back)
    value = chunk(pos)
    yield
    a.wait_recv()
    b.wait_recv()
    done(value + got[3].astype(f32) + got[6].astype(f32))


def kernel(
    gm_in, gt_in, f_in, q_in, bm_in, bt_in, bo, bi, eig, pre,
    gm, gt, f, qi, bm, bt, btt, fit_s, fit_g, qry_s, qry_g, stage, landed, stage_q, landed_q,
    rot, qr, sq_s, sq_g, stage_a, landed_a, s_buf, core_s, core_r, u_s, u_g, stage_b, landed_b,
    u_out, u_mine, p_s, p_g, stage_c, landed_c, send, recv, core_send, core_recv, local,
):
    y, xl, c, z, xh = coords()
    x = xh * 2 + xl
    other = device(y, xl, 1 - c, z, xh)
    along_y = (device(turn(y, 1), xl, c, z, xh), device(turn(y, -1), xl, c, z, xh))
    along_z = (device(y, xl, c, turn(z, 1), xh), device(y, xl, c, turn(z, -1), xh))
    right, left = x_device(x + 1, y, c, z), x_device(x + 3, y, c, z)
    pair_l, pair_h = device(y, 1 - xl, c, z, xh), device(y, xl, c, z, 1 - xh)
    g_to, g_from = device(y, c, xh, z, xl), device(y, xh, xl, z, c)
    g_same = jnp.logical_and(xh == xl, xl == c)
    f_to = device(z, xh, c, y, xl)
    f_same = jnp.logical_and(y == z, xl == xh)

    for who in (other, *along_y, *along_z, right, left, pair_h):
        signal(who)

    @pl.when(jnp.logical_not(g_same))
    def _():
        signal(g_from)

    @pl.when(jnp.logical_not(f_same))
    def _():
        signal(f_to)

    wait_all(10 - g_same.astype(jnp.int32) - f_same.astype(jnp.int32))
    copies = Copies(send, recv)

    g_wait = permute(copies, local.at[0], gm_in, gm.at[xh, y], g_to, g_same)
    t_wait = permute(copies, local.at[1], gt_in, gt.at[y, pl.ds(xh * 16, 16)], g_to, g_same)
    f_wait = permute(copies, local.at[2], f_in, f.at[c, z, xh], f_to, f_same)

    def bm_at(q):
        return bm.at[lax.div(q, 2), lax.rem(q, 2)]

    def bt_at(q):
        return bt.at[lax.rem(q, 2), pl.ds(lax.div(q, 2) * 16, 16)]

    own = [
        pltpu.make_async_copy(bm_in, bm_at(x), local.at[3]),
        pltpu.make_async_copy(bt_in, bt_at(x), local.at[4]),
        pltpu.make_async_copy(q_in, qi.at[y, xl, c], local.at[5]),
    ]
    for copy in own:
        copy.start()
    m_right = copies.start(bm_in, bm_at(x), right)
    m_left = copies.start(bm_in, bm_at(x), left)
    t_right = copies.start(bt_in, bt_at(x), right)
    t_left = copies.start(bt_in, bt_at(x), left)
    q_swap = copies.start(q_in, qi.at[y, xl, c], pair_l)

    forwards = []

    def pass_on(slot):
        def ready(at):
            forwards.append(copies.start(slot(at), slot(at), other))

        return ready

    def around(slot, sign, first=None):
        return gather_stream(copies, y, along_y, sign, slot, pass_on(slot), first)

    own[2].wait()
    q_swap.wait_recv()
    g_wait()
    t_wait()
    far = []

    def over_x():
        x_l, x_r = lax.rem(x + 3, 4), lax.rem(x + 1, 4)
        yield
        m_right.wait_recv()
        half = bm_at(x_l).at[pl.ds(0, 144)]
        far.append(copies.start(half, half, right))
        yield
        m_left.wait_recv()
        half = bm_at(x_r).at[pl.ds(144, 128)]
        far.append(copies.start(half, half, left))
        t_right.wait_recv()
        t_left.wait_recv()
        far.append(copies.start(bt_at(x_l), bt_at(x_l), right))

    run(
        around(lambda at: gm.at[c, at, pl.ds(0, 112)], 1),
        around(lambda at: gm.at[c, at, pl.ds(112, 96)], -1),
        around(lambda at: gt.at[at, pl.ds(c * 16, 16)], 1),
        around(lambda at: qi.at[at, 0, c], 1),
        around(lambda at: qi.at[at, 1, c], -1),
        over_x(),
    )
    own[0].wait()
    own[1].wait()
    for copy in forwards + far:
        copy.wait_recv()
    forwards.clear()
    eye = (
        lax.broadcasted_iota(jnp.int32, (32, 32), 0)
        == lax.broadcasted_iota(jnp.int32, (32, 32), 1)
    ).astype(bf16)
    for b in range(2):
        btt[b] = lax.dot_general(bt[b], eye, TN, preferred_element_type=f32).astype(bf16)

    f_wait()
    f_swap = copies.start(f.at[c, y, xl], f.at[c, y, xl], pair_l)

    def fit_chunk(b):
        def chunk(d):
            part = lax.dot_general(
                bm[0, b], gm[0, d, pl.ds(0, SEQ)], NT, preferred_element_type=f32
            )
            part += lax.dot_general(
                bm[1, b], gm[1, d, pl.ds(0, SEQ)], NT, preferred_element_type=f32
            )
            return part + jnp.dot(btt[b], gt[d], preferred_element_type=f32)[:, :SEQ]

        return chunk

    def query_chunk(d):
        parts = []
        for b in range(2):
            part = lax.dot_general(
                gm[0, d, pl.ds(SEQ, 16)], bm[0, b], NT, preferred_element_type=f32
            )
            part += lax.dot_general(
                gm[1, d, pl.ds(SEQ, 16)], bm[1, b], NT, preferred_element_type=f32
            )
            tail = lax.dot_general(gt[d], bt[b], TN, preferred_element_type=f32)
            parts.append(part + tail[SEQ:TOK])
        return jnp.concatenate(parts, axis=0)

    def fit_done(b):
        def done(total):
            stage[b] = total.astype(bf16)

        return done

    def query_done(total):
        stage_q[0] = total[:16].astype(bf16)
        stage_q[1] = total[16:].astype(bf16)

    run(
        scatter_stream(copies, z, along_z, 1, fit_chunk(0), fit_s.at[0], fit_g.at[0], fit_done(0)),
        scatter_stream(copies, z, along_z, -1, fit_chunk(1), fit_s.at[1], fit_g.at[1], fit_done(1)),
        scatter_stream(copies, z, along_z, 1, query_chunk, qry_s, qry_g, query_done),
        around(lambda at: f.at[c, at, xl], 1),
        around(lambda at: f.at[c, at, 1 - xl], -1, f_swap.wait_recv),
    )
    swap = copies.start(stage.at[1 - xl], landed, pair_l)
    swap_q = copies.start(stage_q.at[1 - xl], landed_q, pair_l)
    rot[xl] = stage[xl]
    qr[z, xh, xl] = stage_q[xl]
    swap_q.wait_recv()
    qr[z, xh, 1 - xl] = landed_q[...]
    q_swap2 = copies.start(qr.at[z, xh], qr.at[z, xh], pair_h)
    swap.wait_recv()
    rot[1 - xl] = landed[...]
    for copy in forwards:
        copy.wait_recv()

    def square_chunk(side):
        def chunk(d):
            first = jnp.dot(rot[0], f[0, d, side], preferred_element_type=f32)
            second = jnp.dot(rot[1], f[1, d, side], preferred_element_type=f32)
            return first * first + second * second

        return chunk

    swaps, sums = [], []

    def far_done(total):
        stage_a[...] = total.astype(bf16)
        swaps.append(copies.start(stage_a, landed_a, pair_h))

    run(
        scatter_stream(
            copies, z, along_z, 1, square_chunk(1 - xh), sq_s.at[0], sq_g.at[0], far_done
        ),
        scatter_stream(
            copies, z, along_z, -1, square_chunk(xh), sq_s.at[1], sq_g.at[1], sums.append
        ),
        gather_stream(copies, z, along_z, 1, lambda at: qr.at[at, xh]),
        gather_stream(
            copies, z, along_z, -1, lambda at: qr.at[at, 1 - xh], None, q_swap2.wait_recv
        ),
    )
    query_sum = lax.dot_general(
        qr[...].reshape(512, PAD), qi[...].reshape(512, 128), TN, preferred_element_type=f32
    )
    swaps[0].wait_recv()
    values = (sums[0] + landed_a[...].astype(f32)) / N_SEQ
    eig[...] = values[:COL]
    s_buf[z, xh] = (query_sum / (values + damping)).astype(bf16)
    s_swap = copies.start(s_buf.at[z, xh], s_buf.at[z, xh], pair_h)

    def across(d, side):
        return pltpu.make_async_remote_copy(
            src_ref=core_s.at[d, side], dst_ref=core_r.at[d, side],
            send_sem=core_send.at[d, side], recv_sem=core_recv.at[d, side],
            device_id=other, device_id_type=pl.DeviceIdType.MESH,
        )

    def to_core(side):
        def ready(d):
            core_s[d, side] = jnp.dot(
                bo[1 - c], s_buf[d, side], preferred_element_type=f32
            ).astype(bf16)
            copy = across(d, side)
            copy.start()
            copies.started.append(copy)

        return ready

    run(
        gather_stream(copies, z, along_z, 1, lambda at: s_buf.at[at, xh], to_core(xh)),
        gather_stream(
            copies, z, along_z, -1, lambda at: s_buf.at[at, 1 - xh], to_core(1 - xh),
            s_swap.wait_recv,
        ),
    )

    def u_chunk(side):
        def chunk(d):
            part = jnp.dot(bo[c], s_buf[d, side], preferred_element_type=f32)
            across(d, side).wait_recv()
            return part + core_r[d, side].astype(f32)

        return chunk

    swaps, sums = [], []

    def u_done(total):
        stage_b[...] = total.astype(bf16)
        swaps.append(copies.start(stage_b, landed_b, pair_l))

    run(
        scatter_stream(copies, y, along_y, 1, u_chunk(1 - xl), u_s.at[0], u_g.at[0], u_done),
        scatter_stream(copies, y, along_y, -1, u_chunk(xl), u_s.at[1], u_g.at[1], sums.append),
    )
    swaps[0].wait_recv()
    u_out[...] = (sums[0] + landed_b[...].astype(f32)).astype(bf16)
    permute(copies, local.at[6], u_out, u_mine, f_to, f_same)()

    def p_chunk(side):
        def chunk(d):
            return lax.dot_general(u_mine[...], bi[2 * d + side], NT, preferred_element_type=f32)

        return chunk

    swaps, sums = [], []

    def p_done(total):
        stage_c[...] = total.astype(bf16)
        swaps.append(copies.start(stage_c, landed_c, pair_h))

    run(
        scatter_stream(copies, z, along_z, 1, p_chunk(1 - xh), p_s.at[0], p_g.at[0], p_done),
        scatter_stream(copies, z, along_z, -1, p_chunk(xh), p_s.at[1], p_g.at[1], sums.append),
    )
    swaps[0].wait_recv()
    pre[...] = (sums[0] + landed_c[...].astype(f32))[:COL].astype(bf16)
    copies.finish()


def per_device(out_grads, layer_inputs, query_grads, query_inputs, basis_out, basis_in):
    shape = jax.ShapeDtypeStruct
    anywhere, vmem = pl.BlockSpec(memory_space=pl.ANY), pl.BlockSpec(memory_space=pltpu.VMEM)
    dma = pltpu.SemaphoreType.DMA

    tokens = jnp.concatenate([out_grads, query_grads], axis=0)
    gm = tokens[:, :MAIN]
    gt = jnp.pad(tokens[:, MAIN:].T, ((0, 12), (0, 48)))
    f = jnp.dot(layer_inputs, basis_in, preferred_element_type=f32).astype(bf16)
    q = jnp.dot(query_inputs, basis_in, preferred_element_type=f32).astype(bf16)
    bm = jnp.pad(basis_out[:MAIN].T, ((0, PAD - COL), (0, 0)))
    bt = jnp.pad(basis_out[MAIN:], ((0, 12), (0, PAD - COL)))
    bo = jnp.pad(
        basis_out.reshape(2, COL, COL), ((0, 0), (0, PAD - COL), (0, PAD - COL))
    )

    def ram(*extent):
        return pltpu.VMEM(extent, bf16)

    def ring(streams, *extent):
        return [ram(*streams, 7, *extent), ram(*streams, 7, *extent)]

    return pl.pallas_call(
        kernel,
        out_shape=[shape((COL, 128), f32), shape((COL, 128), bf16)],
        in_specs=[anywhere] * 6 + [vmem] * 2,
        out_specs=[vmem] * 2,
        scratch_shapes=[
            ram(2, RING, TOK, MAIN),
            ram(RING, 32, 256),
            ram(2, RING, 2, SEQ, 128),
            ram(RING, 2, 2, 16, 128),
            ram(2, 2, PAD, MAIN),
            ram(2, 32, PAD),
            ram(2, PAD, 32),
            *ring((2,), PAD, SEQ),
            *ring((), 32, PAD),
            ram(2, PAD, SEQ),
            ram(PAD, SEQ),
            ram(2, 16, PAD),
            ram(16, PAD),
            ram(2, PAD, SEQ),
            ram(RING, 2, 2, 16, PAD),
            *ring((2,), PAD, 128),
            ram(PAD, 128),
            ram(PAD, 128),
            ram(RING, 2, PAD, 128),
            ram(RING, 2, PAD, 128),
            ram(RING, 2, PAD, 128),
            *ring((2,), PAD, 128),
            ram(PAD, 128),
            ram(PAD, 128),
            ram(PAD, 128),
            ram(PAD, 128),
            *ring((2,), PAD, 128),
            ram(PAD, 128),
            ram(PAD, 128),
            dma((N_SEM,)),
            dma((N_SEM,)),
            dma((RING, 2)),
            dma((RING, 2)),
            dma((7,)),
        ],
        compiler_params=pltpu.CompilerParams(
            collective_id=0, has_side_effects=True, vmem_limit_bytes=56 * 2**20
        ),
    )(gm, gt, f, q, bm, bt, bo, basis_in.reshape(16, 128, 128))


def solution(mesh):
    in_specs = (
        P("dp", "panel"),
        P("dp", None),
        P("dp", "panel"),
        P("dp", None),
        P("panel", "dp"),
        P(None, "panel"),
    )
    out_specs = (P("dp", "panel"), P("dp", "panel"))
    return jax.shard_map(
        per_device, mesh=mesh, in_specs=in_specs, out_specs=out_specs, check_vma=False
    )
```

```python
import jax
import jax.numpy as jnp
from jax import lax
from jax.experimental import pallas as pl
from jax.experimental.pallas import tpu as pltpu
from jax.sharding import PartitionSpec as P

damping = 0.1
bf16 = jnp.bfloat16
f32 = jnp.float32
SEQ = 192
TOK = 208
COL = 258
PAD = 272
MAIN = 512
N_SEQ = 32
RING = 8
NT = (((1,), (1,)), ((), ()))
TN = (((0,), (0,)), ((), ()))
N_SEM = 256


def coords():
    dp, panel = lax.axis_index("dp"), lax.axis_index("panel")
    y, xl, c = lax.div(dp, 4), lax.rem(lax.div(dp, 2), 2), lax.rem(dp, 2)
    return y, xl, c, lax.div(panel, 2), lax.rem(panel, 2)


def device(y, xl, c, z, xh):
    return (y * 4 + xl * 2 + c, z * 2 + xh)


def turn(pos, by):
    return lax.rem(pos + by + RING, RING)


def x_device(x, y, c, z):
    x = lax.rem(x + 4, 4)
    return device(y, lax.rem(x, 2), c, z, lax.div(x, 2))


def signal(who):
    pl.semaphore_signal(
        pltpu.get_barrier_semaphore(), inc=1, device_id=who, device_id_type=pl.DeviceIdType.MESH
    )


def wait_all(count):
    pl.semaphore_wait(pltpu.get_barrier_semaphore(), count)


class Copies:
    def __init__(self, send, recv):
        self.send, self.recv, self.used, self.started = send, recv, 0, []

    def make(self, src, dst, who):
        k = self.used
        self.used += 1
        return pltpu.make_async_remote_copy(
            src_ref=src, dst_ref=dst, send_sem=self.send.at[k], recv_sem=self.recv.at[k],
            device_id=who, device_id_type=pl.DeviceIdType.MESH,
        )

    def start(self, src, dst, who):
        copy = self.make(src, dst, who)
        copy.start()
        self.started.append(copy)
        return copy

    def finish(self):
        for copy in self.started:
            copy.wait_send()


def permute(copies, local_sem, src, dst, who, same):
    copy = copies.make(src, dst, who)
    local = pltpu.make_async_copy(src, dst, local_sem)

    @pl.when(jnp.logical_not(same))
    def _():
        copy.start()

    @pl.when(same)
    def _():
        local.start()

    def wait():
        @pl.when(jnp.logical_not(same))
        def _():
            copy.wait()

        @pl.when(same)
        def _():
            local.wait()

    return wait


def run(*streams):
    live = list(streams)
    while live:
        for stream in list(live):
            try:
                next(stream)
            except StopIteration:
                live.remove(stream)


def gather_stream(copies, pos, ways, sign, slot, ready=None, first=None):
    ahead, back = ways[::sign]
    if first is not None:
        yield
        first()
    a = copies.start(slot(pos), slot(pos), ahead)
    b = copies.start(slot(pos), slot(pos), back)
    if ready is not None:
        ready(pos)
    for t in range(1, 5):
        yield
        at = turn(pos, -sign * t)
        a.wait_recv()
        if t < 4:
            a = copies.start(slot(at), slot(at), ahead)
        if ready is not None:
            ready(at)
        if t < 4:
            yield
            at = turn(pos, sign * t)
            b.wait_recv()
            if t < 3:
                b = copies.start(slot(at), slot(at), back)
            if ready is not None:
                ready(at)


def scatter_stream(copies, pos, ways, sign, chunk, sent, got, done):
    ahead, back = ways[::sign]
    a = b = None
    for t in range(4):
        value = chunk(turn(pos, sign * (4 - t)))
        if t:
            yield
            a.wait_recv()
            value = value + got[t - 1].astype(f32)
        sent[t] = value.astype(bf16)
        a = copies.start(sent.at[t], got.at[t], ahead)
        if t < 3:
            value = chunk(turn(pos, sign * (t - 3)))
            if t:
                yield
                b.wait_recv()
                value = value + got[3 + t].astype(f32)
            sent[4 + t] = value.astype(bf16)
            b = copies.start(sent.at[4 + t], got.at[4 + t], back)
    value = chunk(pos)
    yield
    a.wait_recv()
    b.wait_recv()
    done(value + got[3].astype(f32) + got[6].astype(f32))


def chosen(rows, columns, shift, limit):
    r = lax.broadcasted_iota(jnp.int32, (rows, columns), 0)
    k = lax.broadcasted_iota(jnp.int32, (rows, columns), 1)
    return jnp.logical_and(k == r + shift, r < limit).astype(f32).astype(bf16)


def kernel(
    og, li, qg, ql, bout, bin_, eig, pre,
    gm_in, gt_in, f_in, tt, bo, bia, img,
    gm, gt, f, qi, bm, bt, btt, fit_s, fit_g, qry_s, qry_g, stage, landed, stage_q, landed_q,
    rot, qr, sq_s, sq_g, stage_a, landed_a, s_buf, core_s, core_r, u_s, u_g, stage_b, landed_b,
    u_out, u_mine, send, recv, core_send, core_recv, local,
):
    y, xl, c, z, xh = coords()
    x = xh * 2 + xl
    other = device(y, xl, 1 - c, z, xh)
    along_y = (device(turn(y, 1), xl, c, z, xh), device(turn(y, -1), xl, c, z, xh))
    along_z = (device(y, xl, c, turn(z, 1), xh), device(y, xl, c, turn(z, -1), xh))
    right, left = x_device(x + 1, y, c, z), x_device(x + 3, y, c, z)
    pair_l, pair_h = device(y, 1 - xl, c, z, xh), device(y, xl, c, z, 1 - xh)
    g_to, g_from = device(y, c, xh, z, xl), device(y, xh, xl, z, c)
    g_same = jnp.logical_and(xh == xl, xl == c)
    f_to = device(z, xh, c, y, xl)
    f_same = jnp.logical_and(y == z, xl == xh)

    for who in (other, *along_y, *along_z, right, left, pair_h):
        signal(who)

    @pl.when(jnp.logical_not(g_same))
    def _():
        signal(g_from)

    @pl.when(jnp.logical_not(f_same))
    def _():
        signal(f_to)

    gm_in[pl.ds(0, SEQ)] = og[:, :MAIN]
    gm_in[pl.ds(SEQ, 16)] = qg[:, :MAIN]
    tt[...] = jnp.zeros_like(tt)
    tt[pl.ds(0, SEQ), pl.ds(0, 4)] = og[:, MAIN:]
    tt[pl.ds(SEQ, 16), pl.ds(0, 4)] = qg[:, MAIN:]
    gt_in[...] = lax.dot_general(
        chosen(16, 128, 0, 4), tt[...], NT, preferred_element_type=f32
    ).astype(bf16)

    wait_all(10 - g_same.astype(jnp.int32) - f_same.astype(jnp.int32))
    copies = Copies(send, recv)

    g_wait = permute(copies, local.at[0], gm_in, gm.at[xh, y], g_to, g_same)
    t_wait = permute(copies, local.at[1], gt_in, gt.at[y, pl.ds(xh * 16, 16)], g_to, g_same)

    quarter = xl * 2 + c

    def bi_at(group, block):
        return bia.at[group, :, pl.ds(pl.multiple_of(block * 128, 128), 128)]

    own_bi = pltpu.make_async_copy(
        bin_.at[pl.ds(quarter * 512, 512)], bi_at(quarter, xh * 8 + z), local.at[3]
    )
    own_bi.start()

    def bm_at(q):
        return bm.at[lax.div(q, 2), lax.rem(q, 2)]

    def bt_at(q):
        return bt.at[lax.rem(q, 2), pl.ds(lax.div(q, 2) * 16, 16)]

    bm[xh, xl] = lax.dot_general(
        chosen(PAD, COL, 0, COL), bout[pl.ds(0, MAIN)], NT, preferred_element_type=f32
    ).astype(bf16)
    m_right = copies.start(bm_at(x), bm_at(x), right)
    m_left = copies.start(bm_at(x), bm_at(x), left)
    bt_own = bt_at(x)
    bt_own[...] = jnp.zeros((16, PAD), bf16)
    bt_own[pl.ds(0, 4), pl.ds(0, COL)] = bout[pl.ds(MAIN, 4)]
    t_right = copies.start(bt_own, bt_own, right)
    t_left = copies.start(bt_own, bt_own, left)
    qi[y, xl, c] = jnp.dot(ql[...], bin_[...], preferred_element_type=f32).astype(bf16)
    q_swap = copies.start(qi.at[y, xl, c], qi.at[y, xl, c], pair_l)
    f_in[...] = jnp.dot(li[...], bin_[...], preferred_element_type=f32).astype(bf16)
    f_wait = permute(copies, local.at[2], f_in, f.at[c, z, xh], f_to, f_same)

    forwards = []

    def pass_on(slot):
        def ready(at):
            forwards.append(copies.start(slot(at), slot(at), other))

        return ready

    def around(slot, sign, first=None):
        return gather_stream(copies, y, along_y, sign, slot, pass_on(slot), first)

    own_bi.wait()
    q_swap.wait_recv()
    g_wait()
    t_wait()
    far = []

    def over_x():
        x_l, x_r = lax.rem(x + 3, 4), lax.rem(x + 1, 4)
        yield
        m_right.wait_recv()
        half = bm_at(x_l).at[pl.ds(0, 144)]
        far.append(copies.start(half, half, right))
        yield
        m_left.wait_recv()
        half = bm_at(x_r).at[pl.ds(144, 128)]
        far.append(copies.start(half, half, left))
        t_right.wait_recv()
        t_left.wait_recv()
        far.append(copies.start(bt_at(x_l), bt_at(x_l), right))

    run(
        around(lambda at: gm.at[c, at, pl.ds(0, 112)], 1),
        around(lambda at: gm.at[c, at, pl.ds(112, 96)], -1),
        around(lambda at: gt.at[at, pl.ds(c * 16, 16)], 1),
        around(lambda at: qi.at[at, 0, c], 1),
        around(lambda at: qi.at[at, 1, c], -1),
        over_x(),
        gather_stream(
            copies, z, along_z, 1, lambda at: bi_at(quarter, xh * 8 + at).at[pl.ds(0, 256)]
        ),
        gather_stream(
            copies, z, along_z, -1, lambda at: bi_at(quarter, xh * 8 + at).at[pl.ds(256, 256)]
        ),
    )

    def quarter_at(q, low=0, count=512):
        lanes = pl.ds(pl.multiple_of(lax.div(q, 2) * 1024, 1024), 1024)
        return bia.at[lax.rem(q, 2) * 2 + c, pl.ds(low, count), lanes]

    x_l, x_r, x_f = lax.rem(x + 3, 4), lax.rem(x + 1, 4), lax.rem(x + 2, 4)
    i_right = copies.start(quarter_at(x), quarter_at(x), right)
    i_left = copies.start(quarter_at(x), quarter_at(x), left)
    i_core = [copies.start(quarter_at(x), quarter_at(x), other)]

    for h in range(2):
        bo[h] = jnp.zeros((PAD, PAD), bf16)
        bo[h, :, pl.ds(0, COL)] = jnp.dot(
            chosen(PAD, 2 * COL, h * COL, COL), bout[...], preferred_element_type=f32
        ).astype(bf16)
    for copy in forwards + far:
        copy.wait_recv()
    forwards.clear()
    eye = (
        lax.broadcasted_iota(jnp.int32, (32, 32), 0)
        == lax.broadcasted_iota(jnp.int32, (32, 32), 1)
    ).astype(bf16)
    for b in range(2):
        btt[b] = lax.dot_general(bt[b], eye, TN, preferred_element_type=f32).astype(bf16)

    f_wait()
    f_swap = copies.start(f.at[c, y, xl], f.at[c, y, xl], pair_l)

    def fit_chunk(b):
        def chunk(d):
            part = lax.dot_general(
                bm[0, b], gm[0, d, pl.ds(0, SEQ)], NT, preferred_element_type=f32
            )
            part += lax.dot_general(
                bm[1, b], gm[1, d, pl.ds(0, SEQ)], NT, preferred_element_type=f32
            )
            return part + jnp.dot(btt[b], gt[d], preferred_element_type=f32)[:, :SEQ]

        return chunk

    def query_chunk(d):
        parts = []
        for b in range(2):
            part = lax.dot_general(
                gm[0, d, pl.ds(SEQ, 16)], bm[0, b], NT, preferred_element_type=f32
            )
            part += lax.dot_general(
                gm[1, d, pl.ds(SEQ, 16)], bm[1, b], NT, preferred_element_type=f32
            )
            tail = lax.dot_general(gt[d], bt[b], TN, preferred_element_type=f32)
            parts.append(part + tail[SEQ:TOK])
        return jnp.concatenate(parts, axis=0)

    def fit_done(b):
        def done(total):
            stage[b] = total.astype(bf16)

        return done

    def query_done(total):
        stage_q[0] = total[:16].astype(bf16)
        stage_q[1] = total[16:].astype(bf16)

    run(
        scatter_stream(copies, z, along_z, 1, fit_chunk(0), fit_s.at[0], fit_g.at[0], fit_done(0)),
        scatter_stream(copies, z, along_z, -1, fit_chunk(1), fit_s.at[1], fit_g.at[1], fit_done(1)),
        scatter_stream(copies, z, along_z, 1, query_chunk, qry_s, qry_g, query_done),
        around(lambda at: f.at[c, at, xl], 1),
        around(lambda at: f.at[c, at, 1 - xl], -1, f_swap.wait_recv),
    )
    swap = copies.start(stage.at[1 - xl], landed, pair_l)
    swap_q = copies.start(stage_q.at[1 - xl], landed_q, pair_l)
    rot[xl] = stage[xl]
    qr[z, xh, xl] = stage_q[xl]
    swap_q.wait_recv()
    qr[z, xh, 1 - xl] = landed_q[...]
    q_swap2 = copies.start(qr.at[z, xh], qr.at[z, xh], pair_h)
    swap.wait_recv()
    rot[1 - xl] = landed[...]
    for copy in forwards:
        copy.wait_recv()
    i_right.wait_recv()
    i_far = [copies.start(quarter_at(x_l, 0, 256), quarter_at(x_l, 0, 256), right)]
    i_left.wait_recv()
    i_far.append(copies.start(quarter_at(x_r, 256, 256), quarter_at(x_r, 256, 256), left))
    for q in (x_l, x_r):
        i_core.append(copies.start(quarter_at(q), quarter_at(q), other))

    def square_chunk(side):
        def chunk(d):
            first = jnp.dot(rot[0], f[0, d, side], preferred_element_type=f32)
            second = jnp.dot(rot[1], f[1, d, side], preferred_element_type=f32)
            return first * first + second * second

        return chunk

    swaps, sums = [], []

    def far_done(total):
        stage_a[...] = total.astype(bf16)
        swaps.append(copies.start(stage_a, landed_a, pair_h))

    run(
        scatter_stream(
            copies, z, along_z, 1, square_chunk(1 - xh), sq_s.at[0], sq_g.at[0], far_done
        ),
        scatter_stream(
            copies, z, along_z, -1, square_chunk(xh), sq_s.at[1], sq_g.at[1], sums.append
        ),
        gather_stream(copies, z, along_z, 1, lambda at: qr.at[at, xh]),
        gather_stream(
            copies, z, along_z, -1, lambda at: qr.at[at, 1 - xh], None, q_swap2.wait_recv
        ),
    )
    query_sum = lax.dot_general(
        qr[...].reshape(512, PAD), qi[...].reshape(512, 128), TN, preferred_element_type=f32
    )
    for copy in i_far:
        copy.wait_recv()
    i_core.append(copies.start(quarter_at(x_f), quarter_at(x_f), other))
    swaps[0].wait_recv()
    values = (sums[0] + landed_a[...].astype(f32)) / N_SEQ
    eig[...] = values[:COL]

    def s_at(side, at):
        return s_buf.at[:, pl.ds(pl.multiple_of((side * 8 + at) * 128, 128), 128)]

    s_own = s_at(xh, z)
    s_own[...] = (query_sum / (values + damping)).astype(bf16)
    s_swap = copies.start(s_own, s_own, pair_h)
    run(
        gather_stream(copies, z, along_z, 1, lambda at: s_at(xh, at)),
        gather_stream(
            copies, z, along_z, -1, lambda at: s_at(1 - xh, at), None, s_swap.wait_recv
        ),
    )
    for copy in i_core:
        copy.wait_recv()

    def image(group, carry):
        value = lax.dot_general(s_buf[...], bia[group], NT, preferred_element_type=f32)
        for j in range(4):
            img[group * 4 + j] = value[:, j * 128 : (j + 1) * 128].astype(bf16)
        return carry

    lax.fori_loop(0, 4, image, 0)

    def across(d, side):
        return pltpu.make_async_remote_copy(
            src_ref=core_s.at[d, side], dst_ref=core_r.at[d, side],
            send_sem=core_send.at[d, side], recv_sem=core_recv.at[d, side],
            device_id=other, device_id_type=pl.DeviceIdType.MESH,
        )

    for by in (4, -3, 3, -2, 2, -1, 1, 0):
        d = turn(y, by)
        for side in range(2):
            core_s[d, side] = jnp.dot(
                bo[1 - c], img[2 * d + side], preferred_element_type=f32
            ).astype(bf16)
            copy = across(d, side)
            copy.start()
            copies.started.append(copy)

    def u_chunk(side):
        def chunk(d):
            part = jnp.dot(bo[c], img[2 * d + side], preferred_element_type=f32)
            across(d, side).wait_recv()
            return part + core_r[d, side].astype(f32)

        return chunk

    swaps, sums = [], []

    def u_done(total):
        stage_b[...] = total.astype(bf16)
        swaps.append(copies.start(stage_b, landed_b, pair_l))

    run(
        scatter_stream(copies, y, along_y, 1, u_chunk(1 - xl), u_s.at[0], u_g.at[0], u_done),
        scatter_stream(copies, y, along_y, -1, u_chunk(xl), u_s.at[1], u_g.at[1], sums.append),
    )
    swaps[0].wait_recv()
    u_out[...] = (sums[0] + landed_b[...].astype(f32)).astype(bf16)
    permute(copies, local.at[4], u_out, u_mine, f_to, f_same)()
    pre[...] = u_mine[pl.ds(0, COL)]
    copies.finish()


def per_device(out_grads, layer_inputs, query_grads, query_inputs, basis_out, basis_in):
    shape = jax.ShapeDtypeStruct
    vmem = pl.BlockSpec(memory_space=pltpu.VMEM)
    dma = pltpu.SemaphoreType.DMA

    def ram(*extent):
        return pltpu.VMEM(extent, bf16)

    def ring(streams, *extent):
        return [ram(*streams, 7, *extent), ram(*streams, 7, *extent)]

    return pl.pallas_call(
        kernel,
        out_shape=[shape((COL, 128), f32), shape((COL, 128), bf16)],
        in_specs=[vmem] * 6,
        out_specs=[vmem] * 2,
        scratch_shapes=[
            ram(TOK, MAIN),
            ram(16, 256),
            ram(SEQ, 128),
            ram(256, 128),
            ram(2, PAD, PAD),
            ram(4, 512, 2048),
            ram(16, PAD, 128),
            ram(2, RING, TOK, MAIN),
            ram(RING, 32, 256),
            ram(2, RING, 2, SEQ, 128),
            ram(RING, 2, 2, 16, 128),
            ram(2, 2, PAD, MAIN),
            ram(2, 32, PAD),
            ram(2, PAD, 32),
            *ring((2,), PAD, SEQ),
            *ring((), 32, PAD),
            ram(2, PAD, SEQ),
            ram(PAD, SEQ),
            ram(2, 16, PAD),
            ram(16, PAD),
            ram(2, PAD, SEQ),
            ram(RING, 2, 2, 16, PAD),
            *ring((2,), PAD, 128),
            ram(PAD, 128),
            ram(PAD, 128),
            ram(PAD, 2048),
            ram(RING, 2, PAD, 128),
            ram(RING, 2, PAD, 128),
            *ring((2,), PAD, 128),
            ram(PAD, 128),
            ram(PAD, 128),
            ram(PAD, 128),
            ram(PAD, 128),
            dma((N_SEM,)),
            dma((N_SEM,)),
            dma((RING, 2)),
            dma((RING, 2)),
            dma((5,)),
        ],
        compiler_params=pltpu.CompilerParams(
            collective_id=0, has_side_effects=True, vmem_limit_bytes=56 * 2**20
        ),
    )(out_grads, layer_inputs, query_grads, query_inputs, basis_out, basis_in)


def solution(mesh):
    in_specs = (
        P("dp", "panel"),
        P("dp", None),
        P("dp", "panel"),
        P("dp", None),
        P("panel", "dp"),
        P(None, "panel"),
    )
    out_specs = (P("dp", "panel"), P("dp", "panel"))
    return jax.shard_map(
        per_device, mesh=mesh, in_specs=in_specs, out_specs=out_specs, check_vma=False
    )
```

```python
import jax
import jax.numpy as jnp
from jax import lax
from jax.experimental import pallas as pl
from jax.experimental.pallas import tpu as pltpu
from jax.sharding import PartitionSpec as P

damping = 0.1
bf16 = jnp.bfloat16
f32 = jnp.float32
SEQ = 192
TOK = 208
COL = 258
PAD = 272
MAIN = 512
N_SEQ = 32
RING = 8
PARTS = ((0, 144), (144, 128))
NT = (((1,), (1,)), ((), ()))
TN = (((0,), (0,)), ((), ()))
N_SEM = 320


def coords():
    dp, panel = lax.axis_index("dp"), lax.axis_index("panel")
    y, xl, c = lax.div(dp, 4), lax.rem(lax.div(dp, 2), 2), lax.rem(dp, 2)
    return y, xl, c, lax.div(panel, 2), lax.rem(panel, 2)


def device(y, xl, c, z, xh):
    return (y * 4 + xl * 2 + c, z * 2 + xh)


def turn(pos, by):
    return lax.rem(pos + by + RING, RING)


def x_device(x, y, c, z):
    x = lax.rem(x + 4, 4)
    return device(y, lax.rem(x, 2), c, z, lax.div(x, 2))


def signal(who):
    pl.semaphore_signal(
        pltpu.get_barrier_semaphore(), inc=1, device_id=who, device_id_type=pl.DeviceIdType.MESH
    )


def wait_all(count):
    pl.semaphore_wait(pltpu.get_barrier_semaphore(), count)


class Copies:
    def __init__(self, send, recv):
        self.send, self.recv, self.used, self.started = send, recv, 0, []

    def make(self, src, dst, who):
        k = self.used
        self.used += 1
        return pltpu.make_async_remote_copy(
            src_ref=src, dst_ref=dst, send_sem=self.send.at[k], recv_sem=self.recv.at[k],
            device_id=who, device_id_type=pl.DeviceIdType.MESH,
        )

    def start(self, src, dst, who):
        copy = self.make(src, dst, who)
        copy.start()
        self.started.append(copy)
        return copy

    def finish(self):
        for copy in self.started:
            copy.wait_send()


def permute(copies, local_sem, src, dst, who, same):
    copy = copies.make(src, dst, who)
    local = pltpu.make_async_copy(src, dst, local_sem)

    @pl.when(jnp.logical_not(same))
    def _():
        copy.start()

    @pl.when(same)
    def _():
        local.start()

    def wait():
        @pl.when(jnp.logical_not(same))
        def _():
            copy.wait()

        @pl.when(same)
        def _():
            local.wait()

    return wait


def run(*streams):
    live = list(streams)
    while live:
        for stream in list(live):
            try:
                next(stream)
            except StopIteration:
                live.remove(stream)


def gather_stream(copies, pos, ways, sign, slot, ready=None, first=None):
    ahead, back = ways[::sign]
    if first is not None:
        yield
        first()
    a = copies.start(slot(pos), slot(pos), ahead)
    b = copies.start(slot(pos), slot(pos), back)
    if ready is not None:
        ready(pos)
    for t in range(1, 5):
        yield
        at = turn(pos, -sign * t)
        a.wait_recv()
        if t < 4:
            a = copies.start(slot(at), slot(at), ahead)
        if ready is not None:
            ready(at)
        if t < 4:
            yield
            at = turn(pos, sign * t)
            b.wait_recv()
            if t < 3:
                b = copies.start(slot(at), slot(at), back)
            if ready is not None:
                ready(at)


def scatter_stream(copies, pos, ways, sign, chunk, sent, got, done):
    ahead, back = ways[::sign]
    a = b = None
    for t in range(4):
        value = chunk(turn(pos, 4 - t) if sign > 0 else turn(pos, t - 4), 4 - t)
        if t:
            yield
            a.wait_recv()
            value = value + got[t - 1].astype(f32)
        sent[t] = value.astype(bf16)
        a = copies.start(sent.at[t], got.at[t], ahead)
        if t < 3:
            value = chunk(turn(pos, t - 3) if sign > 0 else turn(pos, 3 - t), t - 3)
            if t:
                yield
                b.wait_recv()
                value = value + got[3 + t].astype(f32)
            sent[4 + t] = value.astype(bf16)
            b = copies.start(sent.at[4 + t], got.at[4 + t], back)
    value = chunk(pos, 0)
    yield
    a.wait_recv()
    b.wait_recv()
    done(value + got[3].astype(f32) + got[6].astype(f32))


def chosen(rows, columns, shift, limit):
    r = lax.broadcasted_iota(jnp.int32, (rows, columns), 0)
    k = lax.broadcasted_iota(jnp.int32, (rows, columns), 1)
    return jnp.logical_and(k == r + shift, r < limit).astype(f32).astype(bf16)


def kernel(
    og, li, qg, ql, bout, bin_, eig, pre,
    gm_in, gt_in, f_in, tt, bo, bia, img,
    gm, gt, f, qi, bm, bt, btt, fit_s, fit_g, stage, landed, rot, qr, sq_s, sq_g, stage_a, landed_a, s_buf, core_s, core_r, u_s, u_g, stage_b, landed_b,
    u_out, u_mine, send, recv, core_send, core_recv, local,
):
    y, xl, c, z, xh = coords()
    x = xh * 2 + xl
    other = device(y, xl, 1 - c, z, xh)
    along_y = (device(turn(y, 1), xl, c, z, xh), device(turn(y, -1), xl, c, z, xh))
    along_z = (device(y, xl, c, turn(z, 1), xh), device(y, xl, c, turn(z, -1), xh))
    right, left = x_device(x + 1, y, c, z), x_device(x + 3, y, c, z)
    pair_l, pair_h = device(y, 1 - xl, c, z, xh), device(y, xl, c, z, 1 - xh)
    g_to, g_from = device(y, c, xh, z, xl), device(y, xh, xl, z, c)
    g_same = jnp.logical_and(xh == xl, xl == c)
    f_to = device(z, xh, c, y, xl)
    f_same = jnp.logical_and(y == z, xl == xh)

    for who in (other, *along_y, *along_z, right, left, pair_h):
        signal(who)

    @pl.when(jnp.logical_not(g_same))
    def _():
        signal(g_from)

    @pl.when(jnp.logical_not(f_same))
    def _():
        signal(f_to)

    gm_in[pl.ds(0, SEQ)] = og[:, :MAIN]
    gm_in[pl.ds(SEQ, 16)] = qg[:, :MAIN]
    tt[...] = jnp.zeros_like(tt)
    tt[pl.ds(0, SEQ), pl.ds(0, 4)] = og[:, MAIN:]
    tt[pl.ds(SEQ, 16), pl.ds(0, 4)] = qg[:, MAIN:]
    gt_in[...] = lax.dot_general(
        chosen(16, 128, 0, 4), tt[...], NT, preferred_element_type=f32
    ).astype(bf16)

    wait_all(10 - g_same.astype(jnp.int32) - f_same.astype(jnp.int32))
    copies = Copies(send, recv)

    g_wait = permute(copies, local.at[0], gm_in, gm.at[xh, y], g_to, g_same)
    t_wait = permute(copies, local.at[1], gt_in, gt.at[y, pl.ds(xh * 16, 16)], g_to, g_same)

    quarter = xl * 2 + c

    def bi_at(group, block):
        return bia.at[group, :, pl.ds(pl.multiple_of(block * 128, 128), 128)]

    own_bi = pltpu.make_async_copy(
        bin_.at[pl.ds(quarter * 512, 512)], bi_at(quarter, xh * 8 + z), local.at[3]
    )
    own_bi.start()

    def bm_at(q):
        return bm.at[lax.div(q, 2), lax.rem(q, 2)]

    def bt_at(q):
        return bt.at[lax.rem(q, 2), pl.ds(lax.div(q, 2) * 16, 16)]

    bm[xh, xl] = lax.dot_general(
        chosen(PAD, COL, 0, COL), bout[pl.ds(0, MAIN)], NT, preferred_element_type=f32
    ).astype(bf16)
    bt_own = bt_at(x)
    bt_own[...] = jnp.zeros((16, PAD), bf16)
    bt_own[pl.ds(0, 4), pl.ds(0, COL)] = bout[pl.ds(MAIN, 4)]
    qi[y, xl, c] = jnp.dot(ql[...], bin_[...], preferred_element_type=f32).astype(bf16)
    q_swap = copies.start(qi.at[y, xl, c], qi.at[y, xl, c], pair_l)
    f_in[...] = jnp.dot(li[...], bin_[...], preferred_element_type=f32).astype(bf16)
    f_wait = permute(copies, local.at[2], f_in, f.at[c, z, xh], f_to, f_same)

    forwards = []

    def pass_on(slot):
        def ready(at):
            forwards.append(copies.start(slot(at), slot(at), other))

        return ready

    def around(slot, sign, first=None):
        return gather_stream(copies, y, along_y, sign, slot, pass_on(slot), first)

    own_bi.wait()
    q_swap.wait_recv()
    g_wait()
    t_wait()
    m_right = copies.start(bm_at(x), bm_at(x), right)
    m_left = copies.start(bm_at(x), bm_at(x), left)
    t_right = copies.start(bt_own, bt_own, right)
    t_left = copies.start(bt_own, bt_own, left)
    far = []

    def over_x():
        x_l, x_r = lax.rem(x + 3, 4), lax.rem(x + 1, 4)
        yield
        m_right.wait_recv()
        half = bm_at(x_l).at[pl.ds(0, 144)]
        far.append(copies.start(half, half, right))
        yield
        m_left.wait_recv()
        half = bm_at(x_r).at[pl.ds(144, 128)]
        far.append(copies.start(half, half, left))
        t_right.wait_recv()
        t_left.wait_recv()
        far.append(copies.start(bt_at(x_l), bt_at(x_l), right))

    run(
        around(lambda at: gm.at[c, at, pl.ds(0, 112)], 1),
        around(lambda at: gm.at[c, at, pl.ds(112, 96)], -1),
        around(lambda at: gt.at[at, pl.ds(c * 16, 16)], 1),
        around(lambda at: qi.at[at, 0, c], 1),
        around(lambda at: qi.at[at, 1, c], -1),
        over_x(),
        gather_stream(
            copies, z, along_z, 1, lambda at: bi_at(quarter, xh * 8 + at).at[pl.ds(0, 256)]
        ),
        gather_stream(
            copies, z, along_z, -1, lambda at: bi_at(quarter, xh * 8 + at).at[pl.ds(256, 256)]
        ),
    )

    def quarter_at(q, low=0, count=512):
        lanes = pl.ds(pl.multiple_of(lax.div(q, 2) * 1024, 1024), 1024)
        return bia.at[lax.rem(q, 2) * 2 + c, pl.ds(low, count), lanes]

    x_l, x_r, x_f = lax.rem(x + 3, 4), lax.rem(x + 1, 4), lax.rem(x + 2, 4)
    i_right = copies.start(quarter_at(x), quarter_at(x), right)
    i_left = copies.start(quarter_at(x), quarter_at(x), left)
    i_core = [copies.start(quarter_at(x), quarter_at(x), other)]

    for h in range(2):
        bo[h] = jnp.zeros((PAD, PAD), bf16)
        bo[h, :, pl.ds(0, COL)] = jnp.dot(
            chosen(PAD, 2 * COL, h * COL, COL), bout[...], preferred_element_type=f32
        ).astype(bf16)
    for copy in forwards + far:
        copy.wait_recv()
    forwards.clear()
    eye = (
        lax.broadcasted_iota(jnp.int32, (32, 32), 0)
        == lax.broadcasted_iota(jnp.int32, (32, 32), 1)
    ).astype(bf16)
    for b in range(2):
        btt[b] = lax.dot_general(bt[b], eye, TN, preferred_element_type=f32).astype(bf16)

    f_wait()
    f_swap = copies.start(f.at[c, y, xl], f.at[c, y, xl], pair_l)

    def fit_stream(b, part):
        low, count = PARTS[part]

        def chunk(d, by):
            value = lax.dot_general(
                bm[0, b, pl.ds(low, count)], gm[0, d], NT, preferred_element_type=f32
            )
            value += lax.dot_general(
                bm[1, b, pl.ds(low, count)], gm[1, d], NT, preferred_element_type=f32
            )
            tail = jnp.dot(btt[b, pl.ds(low, count)], gt[d], preferred_element_type=f32)
            return value + tail[:, :TOK]

        def done(total):
            stage[b, pl.ds(low, count)] = total.astype(bf16)

        return scatter_stream(
            copies, z, along_z, 1 - 2 * b, chunk,
            fit_s.at[b, :, pl.ds(low, count)], fit_g.at[b, :, pl.ds(low, count)], done,
        )

    run(
        fit_stream(0, 0), fit_stream(1, 0), fit_stream(0, 1), fit_stream(1, 1),
        around(lambda at: f.at[c, at, xl], 1),
        around(lambda at: f.at[c, at, 1 - xl], -1, f_swap.wait_recv),
    )
    swap = copies.start(stage.at[1 - xl], landed, pair_l)
    rot[xl] = stage[xl]
    swap.wait_recv()
    rot[1 - xl] = landed[...]
    for h in range(2):
        qr[z, xh, h] = lax.dot_general(
            chosen(16, TOK, SEQ, 16), rot[h], NT, preferred_element_type=f32
        ).astype(bf16)
    q_swap2 = copies.start(qr.at[z, xh], qr.at[z, xh], pair_h)
    for copy in forwards:
        copy.wait_recv()
    i_far = []

    def bi_over_x():
        for _ in range(3):
            yield
        i_right.wait_recv()
        i_far.append(copies.start(quarter_at(x_l, 0, 256), quarter_at(x_l, 0, 256), right))
        i_left.wait_recv()
        i_far.append(copies.start(quarter_at(x_r, 256, 256), quarter_at(x_r, 256, 256), left))
        for q in (x_l, x_r):
            i_core.append(copies.start(quarter_at(q), quarter_at(q), other))

    def bi_far():
        for _ in range(3):
            yield
        for copy in i_far:
            copy.wait_recv()
        i_core.append(copies.start(quarter_at(x_f), quarter_at(x_f), other))

    swaps, sums = {}, {}

    def square_stream(near, part):
        low, count = PARTS[part]
        side = xh if near else 1 - xh

        def chunk(d, by):
            first = jnp.dot(
                rot[0, pl.ds(low, count), pl.ds(0, SEQ)], f[0, d, side],
                preferred_element_type=f32,
            )
            second = jnp.dot(
                rot[1, pl.ds(low, count), pl.ds(0, SEQ)], f[1, d, side],
                preferred_element_type=f32,
            )
            return first * first + second * second

        def done(total):
            if near:
                sums[part] = total
            else:
                half = stage_a.at[pl.ds(low, count)]
                half[...] = total.astype(bf16)
                swaps[part] = copies.start(half, landed_a.at[pl.ds(low, count)], pair_h)

        return scatter_stream(
            copies, z, along_z, -1 if near else 1, chunk,
            sq_s.at[near, :, pl.ds(low, count)], sq_g.at[near, :, pl.ds(low, count)], done,
        )

    run(
        square_stream(0, 0), square_stream(1, 0), square_stream(0, 1), square_stream(1, 1),
        gather_stream(copies, z, along_z, 1, lambda at: qr.at[at, xh]),
        gather_stream(
            copies, z, along_z, -1, lambda at: qr.at[at, 1 - xh], None, q_swap2.wait_recv
        ),
        bi_over_x(),
    )
    query_sum = lax.dot_general(
        qr[...].reshape(512, PAD), qi[...].reshape(512, 128), TN, preferred_element_type=f32
    )
    def s_at(side, at, part):
        low, count = PARTS[part]
        lanes = pl.ds(pl.multiple_of((side * 8 + at) * 128, 128), 128)
        return s_buf.at[pl.ds(low, count), lanes]

    def s_streams(part):
        low, count = PARTS[part]
        swaps[part].wait_recv()
        values = (sums[part] + landed_a[pl.ds(low, count)].astype(f32)) / N_SEQ
        kept = min(count, COL - low)
        eig[pl.ds(low, kept)] = values[:kept]
        own = s_at(xh, z, part)
        own[...] = (query_sum[low : low + count] / (values + damping)).astype(bf16)
        swap = copies.start(own, own, pair_h)
        return (
            gather_stream(copies, z, along_z, 1, lambda at: s_at(xh, at, part)),
            gather_stream(
                copies, z, along_z, -1, lambda at: s_at(1 - xh, at, part), None, swap.wait_recv
            ),
        )

    run(*s_streams(0), *s_streams(1), bi_far())
    for copy in i_core:
        copy.wait_recv()

    def image(group, carry):
        value = lax.dot_general(s_buf[...], bia[group], NT, preferred_element_type=f32)
        for j in range(4):
            img[group * 4 + j] = value[:, j * 128 : (j + 1) * 128].astype(bf16)
        return carry

    lax.fori_loop(0, 4, image, 0)

    def across(d, side):
        return pltpu.make_async_remote_copy(
            src_ref=core_s.at[d, side], dst_ref=core_r.at[d, side],
            send_sem=core_send.at[d, side], recv_sem=core_recv.at[d, side],
            device_id=other, device_id_type=pl.DeviceIdType.MESH,
        )

    for by in (4, -3, 3, -2, 2, -1, 1, 0):
        d = turn(y, by)
        for side in range(2):
            core_s[d, side] = jnp.dot(
                bo[1 - c], img[2 * d + side], preferred_element_type=f32
            ).astype(bf16)
            copy = across(d, side)
            copy.start()
            copies.started.append(copy)

    swaps, sums, seen = {}, {}, set()

    def u_stream(near, part):
        low, count = PARTS[part]
        side = xl if near else 1 - xl

        def chunk(d, by):
            value = jnp.dot(
                bo[c, pl.ds(low, count)], img[2 * d + side], preferred_element_type=f32
            )
            if (near, by) not in seen:
                seen.add((near, by))
                across(d, side).wait_recv()
            return value + core_r[d, side, pl.ds(low, count)].astype(f32)

        def done(total):
            if near:
                sums[part] = total
            else:
                half = stage_b.at[pl.ds(low, count)]
                half[...] = total.astype(bf16)
                swaps[part] = copies.start(half, landed_b.at[pl.ds(low, count)], pair_l)

        return scatter_stream(
            copies, y, along_y, -1 if near else 1, chunk,
            u_s.at[near, :, pl.ds(low, count)], u_g.at[near, :, pl.ds(low, count)], done,
        )

    run(u_stream(0, 0), u_stream(1, 0), u_stream(0, 1), u_stream(1, 1))
    waits = []
    for part, (low, count) in enumerate(PARTS):
        swaps[part].wait_recv()
        half = u_out.at[pl.ds(low, count)]
        half[...] = (sums[part] + landed_b[pl.ds(low, count)].astype(f32)).astype(bf16)
        waits.append(
            permute(
                copies, local.at[4 + part], half, u_mine.at[pl.ds(low, count)], f_to, f_same
            )
        )
    for wait in waits:
        wait()
    pre[...] = u_mine[pl.ds(0, COL)]
    copies.finish()


def per_device(out_grads, layer_inputs, query_grads, query_inputs, basis_out, basis_in):
    shape = jax.ShapeDtypeStruct
    vmem = pl.BlockSpec(memory_space=pltpu.VMEM)
    dma = pltpu.SemaphoreType.DMA

    def ram(*extent):
        return pltpu.VMEM(extent, bf16)

    def ring(streams, *extent):
        return [ram(*streams, 7, *extent), ram(*streams, 7, *extent)]

    return pl.pallas_call(
        kernel,
        out_shape=[shape((COL, 128), f32), shape((COL, 128), bf16)],
        in_specs=[vmem] * 6,
        out_specs=[vmem] * 2,
        scratch_shapes=[
            ram(TOK, MAIN),
            ram(16, 256),
            ram(SEQ, 128),
            ram(256, 128),
            ram(2, PAD, PAD),
            ram(4, 512, 2048),
            ram(16, PAD, 128),
            ram(2, RING, TOK, MAIN),
            ram(RING, 32, 256),
            ram(2, RING, 2, SEQ, 128),
            ram(RING, 2, 2, 16, 128),
            ram(2, 2, PAD, MAIN),
            ram(2, 32, PAD),
            ram(2, PAD, 32),
            *ring((2,), PAD, TOK),
            ram(2, PAD, TOK),
            ram(PAD, TOK),
            ram(2, PAD, TOK),
            ram(RING, 2, 2, 16, PAD),
            *ring((2,), PAD, 128),
            ram(PAD, 128),
            ram(PAD, 128),
            ram(PAD, 2048),
            ram(RING, 2, PAD, 128),
            ram(RING, 2, PAD, 128),
            *ring((2,), PAD, 128),
            ram(PAD, 128),
            ram(PAD, 128),
            ram(PAD, 128),
            ram(PAD, 128),
            dma((N_SEM,)),
            dma((N_SEM,)),
            dma((RING, 2)),
            dma((RING, 2)),
            dma((6,)),
        ],
        compiler_params=pltpu.CompilerParams(
            collective_id=0, has_side_effects=True, vmem_limit_bytes=56 * 2**20
        ),
    )(out_grads, layer_inputs, query_grads, query_inputs, basis_out, basis_in)


def solution(mesh):
    in_specs = (
        P("dp", "panel"),
        P("dp", None),
        P("dp", "panel"),
        P("dp", None),
        P("panel", "dp"),
        P(None, "panel"),
    )
    out_specs = (P("dp", "panel"), P("dp", "panel"))
    return jax.shard_map(
        per_device, mesh=mesh, in_specs=in_specs, out_specs=out_specs, check_vma=False
    )
```

```python
import jax
import jax.numpy as jnp
from jax import lax
from jax.experimental import pallas as pl
from jax.experimental.pallas import tpu as pltpu
from jax.sharding import PartitionSpec as P

damping = 0.1
bf16 = jnp.bfloat16
f32 = jnp.float32
SEQ = 192
TOK = 208
COL = 258
PAD = 272
MAIN = 512
N_SEQ = 32
RING = 8
PARTS = ((0, 144), (144, 128))
NT = (((1,), (1,)), ((), ()))
TN = (((0,), (0,)), ((), ()))
N_SEM = 320


def coords():
    dp, panel = lax.axis_index("dp"), lax.axis_index("panel")
    y, xl, c = lax.div(dp, 4), lax.rem(lax.div(dp, 2), 2), lax.rem(dp, 2)
    return y, xl, c, lax.div(panel, 2), lax.rem(panel, 2)


def device(y, xl, c, z, xh):
    return (y * 4 + xl * 2 + c, z * 2 + xh)


def turn(pos, by):
    return lax.rem(pos + by + RING, RING)


def x_device(x, y, c, z):
    x = lax.rem(x + 4, 4)
    return device(y, lax.rem(x, 2), c, z, lax.div(x, 2))


def signal(who):
    pl.semaphore_signal(
        pltpu.get_barrier_semaphore(), inc=1, device_id=who, device_id_type=pl.DeviceIdType.MESH
    )


def wait_all(count):
    pl.semaphore_wait(pltpu.get_barrier_semaphore(), count)


class Copies:
    def __init__(self, send, recv):
        self.send, self.recv, self.used, self.started = send, recv, 0, []

    def make(self, src, dst, who):
        k = self.used
        self.used += 1
        return pltpu.make_async_remote_copy(
            src_ref=src, dst_ref=dst, send_sem=self.send.at[k], recv_sem=self.recv.at[k],
            device_id=who, device_id_type=pl.DeviceIdType.MESH,
        )

    def start(self, src, dst, who):
        copy = self.make(src, dst, who)
        copy.start()
        self.started.append(copy)
        return copy

    def finish(self):
        for copy in self.started:
            copy.wait_send()


def permute(copies, local_sem, src, dst, who, same):
    copy = copies.make(src, dst, who)
    local = pltpu.make_async_copy(src, dst, local_sem)

    @pl.when(jnp.logical_not(same))
    def _():
        copy.start()

    @pl.when(same)
    def _():
        local.start()

    def wait():
        @pl.when(jnp.logical_not(same))
        def _():
            copy.wait()

        @pl.when(same)
        def _():
            local.wait()

    return wait


def run(*streams):
    live = list(streams)
    while live:
        for stream in list(live):
            try:
                next(stream)
            except StopIteration:
                live.remove(stream)


class Ahead:
    def __init__(self, make, lead):
        self.make, self.lead, self.made = make, lead, 0

    def need(self, off):
        order = (4, 5, 3, 6, 2, 7, 1, 0)
        last = min(order.index(off % RING) + 1 + self.lead, RING)
        while self.made < last:
            self.make(order[self.made])
            self.made += 1
        return off % RING


def gather_stream(copies, pos, ways, sign, slot, ready=None, first=None):
    ahead, back = ways[::sign]
    if first is not None:
        yield
        first()
    a = copies.start(slot(pos), slot(pos), ahead)
    b = copies.start(slot(pos), slot(pos), back)
    if ready is not None:
        ready(pos)
    for t in range(1, 5):
        yield
        at = turn(pos, -sign * t)
        a.wait_recv()
        if t < 4:
            a = copies.start(slot(at), slot(at), ahead)
        if ready is not None:
            ready(at)
        if t < 4:
            yield
            at = turn(pos, sign * t)
            b.wait_recv()
            if t < 3:
                b = copies.start(slot(at), slot(at), back)
            if ready is not None:
                ready(at)


def scatter_stream(copies, ways, sign, chunk, sent, got, done):
    ahead, back = ways[::sign]
    a = b = None
    for t in range(4):
        value = chunk(sign * (4 - t))
        if t:
            yield
            a.wait_recv()
            value = value + got[t - 1].astype(f32)
        sent[t] = value.astype(bf16)
        a = copies.start(sent.at[t], got.at[t], ahead)
        if t < 3:
            value = chunk(sign * (t - 3))
            if t:
                yield
                b.wait_recv()
                value = value + got[3 + t].astype(f32)
            sent[4 + t] = value.astype(bf16)
            b = copies.start(sent.at[4 + t], got.at[4 + t], back)
    value = chunk(0)
    yield
    a.wait_recv()
    b.wait_recv()
    done(value + got[3].astype(f32) + got[6].astype(f32))


def chosen(rows, columns, shift, limit):
    r = lax.broadcasted_iota(jnp.int32, (rows, columns), 0)
    k = lax.broadcasted_iota(jnp.int32, (rows, columns), 1)
    return jnp.logical_and(k == r + shift, r < limit).astype(f32).astype(bf16)


def kernel(
    og, li, qg, ql, bout, bin_, eig, pre,
    gm_in, gt_in, f_in, tt, bo, bia, img,
    gm, gt, f, qi, bm, bt, btt, fit_s, fit_g, stage, landed, rot, qr, sq_s, sq_g, stage_a, landed_a, s_buf, core_s, core_r, u_s, u_g, stage_b, landed_b,
    u_out, u_mine, send, recv, core_send, core_recv, local,
    fit_v, pair_v,
):
    y, xl, c, z, xh = coords()
    x = xh * 2 + xl
    other = device(y, xl, 1 - c, z, xh)
    along_y = (device(turn(y, 1), xl, c, z, xh), device(turn(y, -1), xl, c, z, xh))
    along_z = (device(y, xl, c, turn(z, 1), xh), device(y, xl, c, turn(z, -1), xh))
    right, left = x_device(x + 1, y, c, z), x_device(x + 3, y, c, z)
    pair_l, pair_h = device(y, 1 - xl, c, z, xh), device(y, xl, c, z, 1 - xh)
    g_to, g_from = device(y, c, xh, z, xl), device(y, xh, xl, z, c)
    g_same = jnp.logical_and(xh == xl, xl == c)
    f_to = device(z, xh, c, y, xl)
    f_same = jnp.logical_and(y == z, xl == xh)

    for who in (other, *along_y, *along_z, right, left, pair_h):
        signal(who)

    @pl.when(jnp.logical_not(g_same))
    def _():
        signal(g_from)

    @pl.when(jnp.logical_not(f_same))
    def _():
        signal(f_to)

    gm_in[pl.ds(0, SEQ)] = og[:, :MAIN]
    gm_in[pl.ds(SEQ, 16)] = qg[:, :MAIN]
    tt[...] = jnp.zeros_like(tt)
    tt[pl.ds(0, SEQ), pl.ds(0, 4)] = og[:, MAIN:]
    tt[pl.ds(SEQ, 16), pl.ds(0, 4)] = qg[:, MAIN:]
    gt_in[...] = lax.dot_general(
        chosen(16, 128, 0, 4), tt[...], NT, preferred_element_type=f32
    ).astype(bf16)

    wait_all(10 - g_same.astype(jnp.int32) - f_same.astype(jnp.int32))
    copies = Copies(send, recv)

    g_wait = permute(copies, local.at[0], gm_in, gm.at[xh, y], g_to, g_same)
    t_wait = permute(copies, local.at[1], gt_in, gt.at[y, pl.ds(xh * 16, 16)], g_to, g_same)

    quarter = xl * 2 + c

    def bi_at(block, low=0, count=128):
        return bia.at[quarter, pl.ds(pl.multiple_of(block * 128 + low, 64), count)]

    bi_own = bi_at(xh * 8 + z)
    bi_own[...] = lax.dot_general(
        chosen(128, 128, 0, 128), bin_[pl.ds(pl.multiple_of(quarter * 512, 512), 512)], NT,
        preferred_element_type=f32,
    ).astype(bf16)

    def side_lanes(side):
        return pl.ds(pl.multiple_of(side * 128, 128), 128)

    def f_at(at, side):
        return f.at[c, at, :, side_lanes(side)]

    def bm_at(q):
        return bm.at[lax.div(q, 2), lax.rem(q, 2)]

    def bt_at(q):
        return bt.at[lax.rem(q, 2), pl.ds(lax.div(q, 2) * 16, 16)]

    bm[xh, xl] = lax.dot_general(
        chosen(PAD, COL, 0, COL), bout[pl.ds(0, MAIN)], NT, preferred_element_type=f32
    ).astype(bf16)
    bt_own = bt_at(x)
    bt_own[...] = jnp.zeros((16, PAD), bf16)
    bt_own[pl.ds(0, 4), pl.ds(0, COL)] = bout[pl.ds(MAIN, 4)]
    qi[y, xl, c] = jnp.dot(ql[...], bin_[...], preferred_element_type=f32).astype(bf16)
    q_swap = copies.start(qi.at[y, xl, c], qi.at[y, xl, c], pair_l)
    f_in[...] = jnp.dot(li[...], bin_[...], preferred_element_type=f32).astype(bf16)
    f_wait = permute(copies, local.at[2], f_in, f_at(z, xh), f_to, f_same)

    forwards = []

    def pass_on(slot):
        def ready(at):
            forwards.append(copies.start(slot(at), slot(at), other))

        return ready

    def around(slot, sign, first=None):
        return gather_stream(copies, y, along_y, sign, slot, pass_on(slot), first)

    q_swap.wait_recv()
    g_wait()
    t_wait()
    m_right = copies.start(bm_at(x), bm_at(x), right)
    m_left = copies.start(bm_at(x), bm_at(x), left)
    t_right = copies.start(bt_own, bt_own, right)
    t_left = copies.start(bt_own, bt_own, left)
    far = []

    def over_x():
        x_l, x_r = lax.rem(x + 3, 4), lax.rem(x + 1, 4)
        yield
        m_right.wait_recv()
        half = bm_at(x_l).at[pl.ds(0, 144)]
        far.append(copies.start(half, half, right))
        yield
        m_left.wait_recv()
        half = bm_at(x_r).at[pl.ds(144, 128)]
        far.append(copies.start(half, half, left))
        t_right.wait_recv()
        t_left.wait_recv()
        far.append(copies.start(bt_at(x_l), bt_at(x_l), right))

    run(
        around(lambda at: gm.at[c, at, pl.ds(0, 112)], 1),
        around(lambda at: gm.at[c, at, pl.ds(112, 96)], -1),
        around(lambda at: gt.at[at, pl.ds(c * 16, 16)], 1),
        around(lambda at: qi.at[at, 0, c], 1),
        around(lambda at: qi.at[at, 1, c], -1),
        over_x(),
        gather_stream(
            copies, z, along_z, 1, lambda at: bi_at(xh * 8 + at, 0, 64)
        ),
        gather_stream(
            copies, z, along_z, -1, lambda at: bi_at(xh * 8 + at, 64, 64)
        ),
    )

    def quarter_at(q, low=0, count=1024):
        start = pl.multiple_of(lax.div(q, 2) * 1024 + low, 512)
        return bia.at[lax.rem(q, 2) * 2 + c, pl.ds(start, count)]

    x_l, x_r, x_f = lax.rem(x + 3, 4), lax.rem(x + 1, 4), lax.rem(x + 2, 4)
    i_right = copies.start(quarter_at(x), quarter_at(x), right)
    i_left = copies.start(quarter_at(x), quarter_at(x), left)
    i_core = [copies.start(quarter_at(x), quarter_at(x), other)]

    bo[...] = jnp.zeros_like(bo)
    for row, half in ((0, c), (PAD, 1 - c)):
        bo[pl.ds(row, PAD), pl.ds(0, COL)] = jnp.dot(
            chosen(PAD, 2 * COL, half * COL, COL), bout[...], preferred_element_type=f32
        ).astype(bf16)
    for copy in forwards + far:
        copy.wait_recv()
    forwards.clear()
    eye = (
        lax.broadcasted_iota(jnp.int32, (32, 32), 0)
        == lax.broadcasted_iota(jnp.int32, (32, 32), 1)
    ).astype(bf16)
    for b in range(2):
        btt[b] = lax.dot_general(bt[b], eye, TN, preferred_element_type=f32).astype(bf16)

    f_wait()
    f_swap = copies.start(f_at(y, xl), f_at(y, xl), pair_l)

    def fit_make(off):
        d = turn(z, off)
        value = lax.dot_general(
            bm[0].reshape(2 * PAD, MAIN), gm[0, d], NT, preferred_element_type=f32
        )
        value += lax.dot_general(
            bm[1].reshape(2 * PAD, MAIN), gm[1, d], NT, preferred_element_type=f32
        )
        tail = jnp.dot(btt[...].reshape(2 * PAD, 32), gt[d], preferred_element_type=f32)
        fit_v[off] = value + tail[:, :TOK]

    fit_ahead = Ahead(fit_make, 0)

    def fit_stream(b, part):
        low, count = PARTS[part]

        def chunk(off):
            return fit_v[fit_ahead.need(off), pl.ds(b * PAD + low, count)]

        def done(total):
            stage[b, pl.ds(low, count)] = total.astype(bf16)

        return scatter_stream(
            copies, along_z, 1 - 2 * b, chunk,
            fit_s.at[b, :, pl.ds(low, count)], fit_g.at[b, :, pl.ds(low, count)], done,
        )

    run(
        fit_stream(0, 0), fit_stream(1, 0), fit_stream(0, 1), fit_stream(1, 1),
        around(lambda at: f_at(at, xl), 1),
        around(lambda at: f_at(at, 1 - xl), -1, f_swap.wait_recv),
    )
    swap = copies.start(stage.at[1 - xl], landed, pair_l)
    rot[xl] = stage[xl]
    swap.wait_recv()
    rot[1 - xl] = landed[...]
    for h in range(2):
        qr[z, xh, h] = lax.dot_general(
            chosen(16, TOK, SEQ, 16), rot[h], NT, preferred_element_type=f32
        ).astype(bf16)
    q_swap2 = copies.start(qr.at[z, xh], qr.at[z, xh], pair_h)
    for copy in forwards:
        copy.wait_recv()
    i_far = []

    def bi_over_x():
        for _ in range(3):
            yield
        i_right.wait_recv()
        i_far.append(copies.start(quarter_at(x_l, 0, 512), quarter_at(x_l, 0, 512), right))
        i_left.wait_recv()
        i_far.append(copies.start(quarter_at(x_r, 512, 512), quarter_at(x_r, 512, 512), left))
        for q in (x_l, x_r):
            i_core.append(copies.start(quarter_at(q), quarter_at(q), other))

    def bi_far():
        for _ in range(3):
            yield
        for copy in i_far:
            copy.wait_recv()
        i_core.append(copies.start(quarter_at(x_f), quarter_at(x_f), other))

    swaps, sums = {}, {}

    def square_make(off):
        d = turn(z, off)
        first = jnp.dot(rot[0, :, pl.ds(0, SEQ)], f[0, d], preferred_element_type=f32)
        second = jnp.dot(rot[1, :, pl.ds(0, SEQ)], f[1, d], preferred_element_type=f32)
        pair_v[off] = first * first + second * second

    square_ahead = Ahead(square_make, 1)

    def square_stream(near, part):
        low, count = PARTS[part]
        side = xh if near else 1 - xh

        def chunk(off):
            return pair_v[square_ahead.need(off), pl.ds(low, count), side_lanes(side)]

        def done(total):
            if near:
                sums[part] = total
            else:
                half = stage_a.at[pl.ds(low, count)]
                half[...] = total.astype(bf16)
                swaps[part] = copies.start(half, landed_a.at[pl.ds(low, count)], pair_h)

        return scatter_stream(
            copies, along_z, -1 if near else 1, chunk,
            sq_s.at[near, :, pl.ds(low, count)], sq_g.at[near, :, pl.ds(low, count)], done,
        )

    run(
        square_stream(0, 0), square_stream(1, 0), square_stream(0, 1), square_stream(1, 1),
        gather_stream(copies, z, along_z, 1, lambda at: qr.at[at, xh]),
        gather_stream(
            copies, z, along_z, -1, lambda at: qr.at[at, 1 - xh], None, q_swap2.wait_recv
        ),
        bi_over_x(),
    )
    query_sum = lax.dot_general(
        qr[...].reshape(512, PAD), qi[...].reshape(512, 128), TN, preferred_element_type=f32
    )
    def s_at(side, at, part):
        low, count = PARTS[part]
        lanes = pl.ds(pl.multiple_of((side * 8 + at) * 128, 128), 128)
        return s_buf.at[pl.ds(low, count), lanes]

    def s_streams(part):
        low, count = PARTS[part]
        swaps[part].wait_recv()
        values = (sums[part] + landed_a[pl.ds(low, count)].astype(f32)) / N_SEQ
        kept = min(count, COL - low)
        eig[pl.ds(low, kept)] = values[:kept]
        own = s_at(xh, z, part)
        own[...] = (query_sum[low : low + count] / (values + damping)).astype(bf16)
        swap = copies.start(own, own, pair_h)
        return (
            gather_stream(copies, z, along_z, 1, lambda at: s_at(xh, at, part)),
            gather_stream(
                copies, z, along_z, -1, lambda at: s_at(1 - xh, at, part), None, swap.wait_recv
            ),
        )

    run(*s_streams(0), *s_streams(1), bi_far())
    for copy in i_core:
        copy.wait_recv()

    def image(group, carry):
        value = jnp.dot(s_buf[...], bia[group], preferred_element_type=f32)
        img[group * 2] = value[:, :256].astype(bf16)
        img[group * 2 + 1] = value[:, 256:].astype(bf16)
        return carry

    lax.fori_loop(0, 4, image, 0)

    def across(d):
        return pltpu.make_async_remote_copy(
            src_ref=core_s.at[d], dst_ref=core_r.at[d],
            send_sem=core_send.at[d], recv_sem=core_recv.at[d],
            device_id=other, device_id_type=pl.DeviceIdType.MESH,
        )

    def u_make(off):
        d = turn(y, off)
        value = jnp.dot(bo[...], img[d], preferred_element_type=f32)
        pair_v[off] = value[:PAD]
        core_s[d] = value[PAD:].astype(bf16)
        copy = across(d)
        copy.start()
        copies.started.append(copy)

    u_ahead = Ahead(u_make, 3)
    swaps, sums, seen = {}, {}, set()

    def u_stream(near, part):
        low, count = PARTS[part]
        side = xl if near else 1 - xl

        def chunk(off):
            key, d = u_ahead.need(off), turn(y, off)
            if key not in seen:
                seen.add(key)
                across(d).wait_recv()
            mine = pair_v[key, pl.ds(low, count), side_lanes(side)]
            return mine + core_r[d, pl.ds(low, count), side_lanes(side)].astype(f32)

        def done(total):
            if near:
                sums[part] = total
            else:
                half = stage_b.at[pl.ds(low, count)]
                half[...] = total.astype(bf16)
                swaps[part] = copies.start(half, landed_b.at[pl.ds(low, count)], pair_l)

        return scatter_stream(
            copies, along_y, -1 if near else 1, chunk,
            u_s.at[near, :, pl.ds(low, count)], u_g.at[near, :, pl.ds(low, count)], done,
        )

    run(u_stream(0, 0), u_stream(1, 0), u_stream(0, 1), u_stream(1, 1))
    waits = []
    for part, (low, count) in enumerate(PARTS):
        swaps[part].wait_recv()
        half = u_out.at[pl.ds(low, count)]
        half[...] = (sums[part] + landed_b[pl.ds(low, count)].astype(f32)).astype(bf16)
        waits.append(
            permute(
                copies, local.at[4 + part], half, u_mine.at[pl.ds(low, count)], f_to, f_same
            )
        )
    for wait in waits:
        wait()
    pre[...] = u_mine[pl.ds(0, COL)]
    copies.finish()


def per_device(out_grads, layer_inputs, query_grads, query_inputs, basis_out, basis_in):
    shape = jax.ShapeDtypeStruct
    vmem = pl.BlockSpec(memory_space=pltpu.VMEM)
    dma = pltpu.SemaphoreType.DMA

    def ram(*extent):
        return pltpu.VMEM(extent, bf16)

    def ring(streams, *extent):
        return [ram(*streams, 7, *extent), ram(*streams, 7, *extent)]

    return pl.pallas_call(
        kernel,
        out_shape=[shape((COL, 128), f32), shape((COL, 128), bf16)],
        in_specs=[vmem] * 6,
        out_specs=[vmem] * 2,
        scratch_shapes=[
            ram(TOK, MAIN),
            ram(16, 256),
            ram(SEQ, 128),
            ram(256, 128),
            ram(2 * PAD, PAD),
            ram(4, 2048, 512),
            ram(RING, PAD, 256),
            ram(2, RING, TOK, MAIN),
            ram(RING, 32, 256),
            ram(2, RING, SEQ, 256),
            ram(RING, 2, 2, 16, 128),
            ram(2, 2, PAD, MAIN),
            ram(2, 32, PAD),
            ram(2, PAD, 32),
            *ring((2,), PAD, TOK),
            ram(2, PAD, TOK),
            ram(PAD, TOK),
            ram(2, PAD, TOK),
            ram(RING, 2, 2, 16, PAD),
            *ring((2,), PAD, 128),
            ram(PAD, 128),
            ram(PAD, 128),
            ram(PAD, 2048),
            ram(RING, PAD, 256),
            ram(RING, PAD, 256),
            *ring((2,), PAD, 128),
            ram(PAD, 128),
            ram(PAD, 128),
            ram(PAD, 128),
            ram(PAD, 128),
            dma((N_SEM,)),
            dma((N_SEM,)),
            dma((RING,)),
            dma((RING,)),
            dma((6,)),
            pltpu.VMEM((RING, 2 * PAD, TOK), f32),
            pltpu.VMEM((RING, PAD, 256), f32),
        ],
        compiler_params=pltpu.CompilerParams(
            collective_id=0, has_side_effects=True, vmem_limit_bytes=56 * 2**20
        ),
    )(out_grads, layer_inputs, query_grads, query_inputs, basis_out, basis_in)


def solution(mesh):
    in_specs = (
        P("dp", "panel"),
        P("dp", None),
        P("dp", "panel"),
        P("dp", None),
        P("panel", "dp"),
        P(None, "panel"),
    )
    out_specs = (P("dp", "panel"), P("dp", "panel"))
    return jax.shard_map(
        per_device, mesh=mesh, in_specs=in_specs, out_specs=out_specs, check_vma=False
    )
```

```python
import jax
import jax.numpy as jnp
from jax import lax
from jax.experimental import pallas as pl
from jax.experimental.pallas import tpu as pltpu
from jax.sharding import PartitionSpec as P

damping = 0.1
bf16 = jnp.bfloat16
f32 = jnp.float32
SEQ = 192
TOK = 208
COL = 258
PAD = 272
MAIN = 512
N_SEQ = 32
RING = 8
PARTS = ((0, 144), (144, 128))
NT = (((1,), (1,)), ((), ()))
TN = (((0,), (0,)), ((), ()))
N_SEM = 320


def coords():
    dp, panel = lax.axis_index("dp"), lax.axis_index("panel")
    y, xl, c = lax.div(dp, 4), lax.rem(lax.div(dp, 2), 2), lax.rem(dp, 2)
    return y, xl, c, lax.div(panel, 2), lax.rem(panel, 2)


def device(y, xl, c, z, xh):
    return (y * 4 + xl * 2 + c, z * 2 + xh)


def turn(pos, by):
    return lax.rem(pos + by + RING, RING)


def x_device(x, y, c, z):
    x = lax.rem(x + 4, 4)
    return device(y, lax.rem(x, 2), c, z, lax.div(x, 2))


def signal(who):
    pl.semaphore_signal(
        pltpu.get_barrier_semaphore(), inc=1, device_id=who, device_id_type=pl.DeviceIdType.MESH
    )


def wait_all(count):
    pl.semaphore_wait(pltpu.get_barrier_semaphore(), count)


class Copies:
    def __init__(self, send, recv):
        self.send, self.recv, self.used, self.started = send, recv, 0, []

    def make(self, src, dst, who):
        k = self.used
        self.used += 1
        return pltpu.make_async_remote_copy(
            src_ref=src, dst_ref=dst, send_sem=self.send.at[k], recv_sem=self.recv.at[k],
            device_id=who, device_id_type=pl.DeviceIdType.MESH,
        )

    def start(self, src, dst, who):
        copy = self.make(src, dst, who)
        copy.start()
        self.started.append(copy)
        return copy

    def finish(self):
        for copy in self.started:
            copy.wait_send()


def permute(copies, local_sem, src, dst, who, same):
    copy = copies.make(src, dst, who)
    local = pltpu.make_async_copy(src, dst, local_sem)

    @pl.when(jnp.logical_not(same))
    def _():
        copy.start()

    @pl.when(same)
    def _():
        local.start()

    def wait():
        @pl.when(jnp.logical_not(same))
        def _():
            copy.wait()

        @pl.when(same)
        def _():
            local.wait()

    return wait


def run(*streams):
    live = list(streams)
    while live:
        for stream in list(live):
            try:
                next(stream)
            except StopIteration:
                live.remove(stream)


class Ahead:
    def __init__(self, make, lead):
        self.make, self.lead, self.made = make, lead, 0

    def need(self, off):
        order = (4, 5, 3, 6, 2, 7, 1, 0)
        last = min(order.index(off % RING) + 1 + self.lead, RING)
        while self.made < last:
            self.make(order[self.made])
            self.made += 1
        return off % RING


def gather_stream(copies, pos, ways, sign, slot, ready=None, first=None):
    ahead, back = ways[::sign]
    if first is not None:
        yield
        first()
    a = copies.start(slot(pos), slot(pos), ahead)
    b = copies.start(slot(pos), slot(pos), back)
    if ready is not None:
        ready(pos)
    for t in range(1, 5):
        yield
        at = turn(pos, -sign * t)
        a.wait_recv()
        if t < 4:
            a = copies.start(slot(at), slot(at), ahead)
        if ready is not None:
            ready(at)
        if t < 4:
            yield
            at = turn(pos, sign * t)
            b.wait_recv()
            if t < 3:
                b = copies.start(slot(at), slot(at), back)
            if ready is not None:
                ready(at)


def scatter_stream(copies, ways, sign, chunk, sent, got, done):
    ahead, back = ways[::sign]
    a = b = None
    for t in range(4):
        value = chunk(sign * (4 - t))
        if t:
            yield
            a.wait_recv()
            value = value + got[t - 1].astype(f32)
        sent[t] = value.astype(bf16)
        a = copies.start(sent.at[t], got.at[t], ahead)
        if t < 3:
            value = chunk(sign * (t - 3))
            if t:
                yield
                b.wait_recv()
                value = value + got[3 + t].astype(f32)
            sent[4 + t] = value.astype(bf16)
            b = copies.start(sent.at[4 + t], got.at[4 + t], back)
    value = chunk(0)
    yield
    a.wait_recv()
    b.wait_recv()
    done(value + got[3].astype(f32) + got[6].astype(f32))


def chosen(rows, columns, shift, limit):
    r = lax.broadcasted_iota(jnp.int32, (rows, columns), 0)
    k = lax.broadcasted_iota(jnp.int32, (rows, columns), 1)
    return jnp.logical_and(k == r + shift, r < limit).astype(f32).astype(bf16)


def kernel(
    og, li, qg, ql, bout, bin_, eig, pre,
    gm_in, gt_in, f_in, tt, bo, bia, img,
    gm, gt, f, qi, bm, bt, btt, fit_s, fit_g, stage, landed, rot, qr, sq_s, sq_g, stage_a, landed_a, s_buf, core_s, core_r, u_s, u_g, stage_b, landed_b,
    u_out, u_mine, send, recv, core_send, core_recv, local,
    fit_v, pair_v,
):
    y, xl, c, z, xh = coords()
    x = xh * 2 + xl
    other = device(y, xl, 1 - c, z, xh)
    along_y = (device(turn(y, 1), xl, c, z, xh), device(turn(y, -1), xl, c, z, xh))
    along_z = (device(y, xl, c, turn(z, 1), xh), device(y, xl, c, turn(z, -1), xh))
    right, left = x_device(x + 1, y, c, z), x_device(x + 3, y, c, z)
    pair_l, pair_h = device(y, 1 - xl, c, z, xh), device(y, xl, c, z, 1 - xh)
    g_to, g_from = device(y, c, xh, z, xl), device(y, xh, xl, z, c)
    g_same = jnp.logical_and(xh == xl, xl == c)
    f_to = device(z, xh, c, y, xl)
    f_same = jnp.logical_and(y == z, xl == xh)

    for who in (other, *along_y, *along_z, right, left, pair_h):
        signal(who)

    @pl.when(jnp.logical_not(g_same))
    def _():
        signal(g_from)

    @pl.when(jnp.logical_not(f_same))
    def _():
        signal(f_to)

    gm_in[pl.ds(0, SEQ)] = og[:, :MAIN]
    gm_in[pl.ds(SEQ, 16)] = qg[:, :MAIN]
    tt[...] = jnp.zeros_like(tt)
    tt[pl.ds(0, SEQ), pl.ds(0, 4)] = og[:, MAIN:]
    tt[pl.ds(SEQ, 16), pl.ds(0, 4)] = qg[:, MAIN:]
    gt_in[...] = lax.dot_general(
        chosen(16, 128, 0, 4), tt[...], NT, preferred_element_type=f32
    ).astype(bf16)

    wait_all(10 - g_same.astype(jnp.int32) - f_same.astype(jnp.int32))
    copies = Copies(send, recv)

    g_wait = permute(copies, local.at[0], gm_in, gm.at[xh, y], g_to, g_same)
    t_wait = permute(copies, local.at[1], gt_in, gt.at[y, pl.ds(xh * 16, 16)], g_to, g_same)

    quarter = xl * 2 + c

    def bi_at(block, low=0, count=128):
        return bia.at[quarter, pl.ds(pl.multiple_of(block * 128 + low, 64), count)]

    bi_own = bi_at(xh * 8 + z)
    bi_own[...] = lax.dot_general(
        chosen(128, 128, 0, 128), bin_[pl.ds(pl.multiple_of(quarter * 512, 512), 512)], NT,
        preferred_element_type=f32,
    ).astype(bf16)

    def side_lanes(side):
        return pl.ds(pl.multiple_of(side * 128, 128), 128)

    def f_at(at, side):
        return f.at[c, at, :, side_lanes(side)]

    def bm_at(q):
        return bm.at[lax.div(q, 2), lax.rem(q, 2)]

    def bt_at(q):
        return bt.at[lax.rem(q, 2), pl.ds(lax.div(q, 2) * 16, 16)]

    bm[xh, xl] = lax.dot_general(
        chosen(PAD, COL, 0, COL), bout[pl.ds(0, MAIN)], NT, preferred_element_type=f32
    ).astype(bf16)
    bt_own = bt_at(x)
    bt_own[...] = jnp.zeros((16, PAD), bf16)
    bt_own[pl.ds(0, 4), pl.ds(0, COL)] = bout[pl.ds(MAIN, 4)]
    qi[y, xl, c] = jnp.dot(ql[...], bin_[...], preferred_element_type=f32).astype(bf16)
    q_swap = copies.start(qi.at[y, xl, c], qi.at[y, xl, c], pair_l)
    f_in[...] = jnp.dot(li[...], bin_[...], preferred_element_type=f32).astype(bf16)
    f_wait = permute(copies, local.at[2], f_in, f_at(z, xh), f_to, f_same)

    forwards = []

    def pass_on(slot):
        def ready(at):
            forwards.append(copies.start(slot(at), slot(at), other))

        return ready

    def around(slot, sign, first=None):
        return gather_stream(copies, y, along_y, sign, slot, pass_on(slot), first)

    g_wait()
    t_wait()
    m_right = copies.start(bm_at(x), bm_at(x), right)
    m_left = copies.start(bm_at(x), bm_at(x), left)
    t_right = copies.start(bt_own, bt_own, right)
    t_left = copies.start(bt_own, bt_own, left)
    far = []

    def over_x():
        x_l, x_r = lax.rem(x + 3, 4), lax.rem(x + 1, 4)
        yield
        m_right.wait_recv()
        half = bm_at(x_l).at[pl.ds(0, 144)]
        far.append(copies.start(half, half, right))
        yield
        m_left.wait_recv()
        half = bm_at(x_r).at[pl.ds(144, 128)]
        far.append(copies.start(half, half, left))
        t_right.wait_recv()
        t_left.wait_recv()
        far.append(copies.start(bt_at(x_l), bt_at(x_l), right))

    run(
        around(lambda at: gm.at[c, at, pl.ds(0, 112)], 1),
        around(lambda at: gm.at[c, at, pl.ds(112, 96)], -1),
        around(lambda at: gt.at[at, pl.ds(c * 16, 16)], 1),
        around(lambda at: qi.at[at, xl, c], 1),
        around(lambda at: qi.at[at, 1 - xl, c], -1, q_swap.wait_recv),
        over_x(),
        gather_stream(
            copies, z, along_z, 1, lambda at: bi_at(xh * 8 + at, 0, 64)
        ),
        gather_stream(
            copies, z, along_z, -1, lambda at: bi_at(xh * 8 + at, 64, 64)
        ),
    )

    def quarter_at(q, low=0, count=1024):
        start = pl.multiple_of(lax.div(q, 2) * 1024 + low, 512)
        return bia.at[lax.rem(q, 2) * 2 + c, pl.ds(start, count)]

    x_l, x_r, x_f = lax.rem(x + 3, 4), lax.rem(x + 1, 4), lax.rem(x + 2, 4)
    f_wait()
    f_swap = copies.start(f_at(y, xl), f_at(y, xl), pair_l)
    i_right = copies.start(quarter_at(x), quarter_at(x), right)
    i_left = copies.start(quarter_at(x), quarter_at(x), left)
    i_core = [copies.start(quarter_at(x), quarter_at(x), other)]

    bo[...] = jnp.zeros_like(bo)
    for row, half in ((0, c), (PAD, 1 - c)):
        bo[pl.ds(row, PAD), pl.ds(0, COL)] = jnp.dot(
            chosen(PAD, 2 * COL, half * COL, COL), bout[...], preferred_element_type=f32
        ).astype(bf16)
    for copy in forwards + far:
        copy.wait_recv()
    forwards.clear()
    eye = (
        lax.broadcasted_iota(jnp.int32, (32, 32), 0)
        == lax.broadcasted_iota(jnp.int32, (32, 32), 1)
    ).astype(bf16)
    for b in range(2):
        btt[b] = lax.dot_general(bt[b], eye, TN, preferred_element_type=f32).astype(bf16)

    def fit_make(off):
        d = turn(z, off)
        value = lax.dot_general(
            bm[0].reshape(2 * PAD, MAIN), gm[0, d], NT, preferred_element_type=f32
        )
        value += lax.dot_general(
            bm[1].reshape(2 * PAD, MAIN), gm[1, d], NT, preferred_element_type=f32
        )
        tail = jnp.dot(btt[...].reshape(2 * PAD, 32), gt[d], preferred_element_type=f32)
        fit_v[off] = value + tail[:, :TOK]

    fit_ahead = Ahead(fit_make, 0)

    fit_swaps = []

    def fit_stream(near, part):
        low, count = PARTS[part]
        row = pl.multiple_of((xl if near else 1 - xl) * PAD + low, 16)

        def chunk(off):
            return fit_v[fit_ahead.need(off), pl.ds(row, count)]

        def done(total):
            if near:
                rot[xl, pl.ds(low, count)] = total.astype(bf16)
            else:
                half = stage.at[pl.ds(low, count)]
                half[...] = total.astype(bf16)
                fit_swaps.append(copies.start(half, landed.at[pl.ds(low, count)], pair_l))

        return scatter_stream(
            copies, along_z, -1 if near else 1, chunk,
            fit_s.at[near, :, pl.ds(low, count)], fit_g.at[near, :, pl.ds(low, count)], done,
        )

    run(
        fit_stream(0, 0), fit_stream(1, 0), fit_stream(0, 1), fit_stream(1, 1),
        around(lambda at: f_at(at, xl), 1),
        around(lambda at: f_at(at, 1 - xl), -1, f_swap.wait_recv),
    )
    for swap in fit_swaps:
        swap.wait_recv()
    rot[1 - xl] = landed[...]
    for h in range(2):
        qr[z, xh, h] = lax.dot_general(
            chosen(16, TOK, SEQ, 16), rot[h], NT, preferred_element_type=f32
        ).astype(bf16)
    q_swap2 = copies.start(qr.at[z, xh], qr.at[z, xh], pair_h)
    for copy in forwards:
        copy.wait_recv()
    i_far = []

    def bi_over_x():
        for _ in range(3):
            yield
        i_right.wait_recv()
        i_far.append(copies.start(quarter_at(x_l, 0, 512), quarter_at(x_l, 0, 512), right))
        i_left.wait_recv()
        i_far.append(copies.start(quarter_at(x_r, 512, 512), quarter_at(x_r, 512, 512), left))
        for q in (x_l, x_r):
            i_core.append(copies.start(quarter_at(q), quarter_at(q), other))

    def bi_far():
        for _ in range(3):
            yield
        for copy in i_far:
            copy.wait_recv()
        i_core.append(copies.start(quarter_at(x_f), quarter_at(x_f), other))

    swaps, sums = {}, {}

    def square_make(off):
        d = turn(z, off)
        first = jnp.dot(rot[0, :, pl.ds(0, SEQ)], f[0, d], preferred_element_type=f32)
        second = jnp.dot(rot[1, :, pl.ds(0, SEQ)], f[1, d], preferred_element_type=f32)
        pair_v[off] = first * first + second * second

    square_ahead = Ahead(square_make, 1)

    def square_stream(near, part):
        low, count = PARTS[part]
        side = xh if near else 1 - xh

        def chunk(off):
            return pair_v[square_ahead.need(off), pl.ds(low, count), side_lanes(side)]

        def done(total):
            if near:
                sums[part] = total
            else:
                half = stage_a.at[pl.ds(low, count)]
                half[...] = total.astype(bf16)
                swaps[part] = copies.start(half, landed_a.at[pl.ds(low, count)], pair_h)

        return scatter_stream(
            copies, along_z, -1 if near else 1, chunk,
            sq_s.at[near, :, pl.ds(low, count)], sq_g.at[near, :, pl.ds(low, count)], done,
        )

    run(
        square_stream(0, 0), square_stream(1, 0), square_stream(0, 1), square_stream(1, 1),
        gather_stream(copies, z, along_z, 1, lambda at: qr.at[at, xh]),
        gather_stream(
            copies, z, along_z, -1, lambda at: qr.at[at, 1 - xh], None, q_swap2.wait_recv
        ),
        bi_over_x(),
    )
    query_sum = lax.dot_general(
        qr[...].reshape(512, PAD), qi[...].reshape(512, 128), TN, preferred_element_type=f32
    )
    def s_at(side, at, part):
        low, count = PARTS[part]
        lanes = pl.ds(pl.multiple_of((side * 8 + at) * 128, 128), 128)
        return s_buf.at[pl.ds(low, count), lanes]

    def s_streams(part):
        low, count = PARTS[part]
        swaps[part].wait_recv()
        values = (sums[part] + landed_a[pl.ds(low, count)].astype(f32)) / N_SEQ
        kept = min(count, COL - low)
        eig[pl.ds(low, kept)] = values[:kept]
        own = s_at(xh, z, part)
        own[...] = (query_sum[low : low + count] / (values + damping)).astype(bf16)
        swap = copies.start(own, own, pair_h)
        return (
            gather_stream(copies, z, along_z, 1, lambda at: s_at(xh, at, part)),
            gather_stream(
                copies, z, along_z, -1, lambda at: s_at(1 - xh, at, part), None, swap.wait_recv
            ),
        )

    run(*s_streams(0), *s_streams(1), bi_far())
    for copy in i_core:
        copy.wait_recv()

    def image(group, carry):
        value = jnp.dot(s_buf[...], bia[group], preferred_element_type=f32)
        img[group * 2] = value[:, :256].astype(bf16)
        img[group * 2 + 1] = value[:, 256:].astype(bf16)
        return carry

    lax.fori_loop(0, 4, image, 0)

    def across(d):
        return pltpu.make_async_remote_copy(
            src_ref=core_s.at[d], dst_ref=core_r.at[d],
            send_sem=core_send.at[d], recv_sem=core_recv.at[d],
            device_id=other, device_id_type=pl.DeviceIdType.MESH,
        )

    def u_make(off):
        d = turn(y, off)
        value = jnp.dot(bo[...], img[d], preferred_element_type=f32)
        pair_v[off] = value[:PAD]
        core_s[d] = value[PAD:].astype(bf16)
        copy = across(d)
        copy.start()
        copies.started.append(copy)

    u_ahead = Ahead(u_make, 3)
    swaps, sums, seen = {}, {}, set()

    def u_stream(near, part):
        low, count = PARTS[part]
        side = xl if near else 1 - xl

        def chunk(off):
            key, d = u_ahead.need(off), turn(y, off)
            if key not in seen:
                seen.add(key)
                across(d).wait_recv()
            mine = pair_v[key, pl.ds(low, count), side_lanes(side)]
            return mine + core_r[d, pl.ds(low, count), side_lanes(side)].astype(f32)

        def done(total):
            if near:
                sums[part] = total
            else:
                half = stage_b.at[pl.ds(low, count)]
                half[...] = total.astype(bf16)
                swaps[part] = copies.start(half, landed_b.at[pl.ds(low, count)], pair_l)

        return scatter_stream(
            copies, along_y, -1 if near else 1, chunk,
            u_s.at[near, :, pl.ds(low, count)], u_g.at[near, :, pl.ds(low, count)], done,
        )

    run(u_stream(0, 0), u_stream(1, 0), u_stream(0, 1), u_stream(1, 1))
    waits = []
    for part, (low, count) in enumerate(PARTS):
        swaps[part].wait_recv()
        half = u_out.at[pl.ds(low, count)]
        half[...] = (sums[part] + landed_b[pl.ds(low, count)].astype(f32)).astype(bf16)
        waits.append(
            permute(
                copies, local.at[4 + part], half, u_mine.at[pl.ds(low, count)], f_to, f_same
            )
        )
    for wait in waits:
        wait()
    pre[...] = u_mine[pl.ds(0, COL)]
    copies.finish()


def per_device(out_grads, layer_inputs, query_grads, query_inputs, basis_out, basis_in):
    shape = jax.ShapeDtypeStruct
    vmem = pl.BlockSpec(memory_space=pltpu.VMEM)
    dma = pltpu.SemaphoreType.DMA

    def ram(*extent):
        return pltpu.VMEM(extent, bf16)

    def ring(streams, *extent):
        return [ram(*streams, 7, *extent), ram(*streams, 7, *extent)]

    return pl.pallas_call(
        kernel,
        out_shape=[shape((COL, 128), f32), shape((COL, 128), bf16)],
        in_specs=[vmem] * 6,
        out_specs=[vmem] * 2,
        scratch_shapes=[
            ram(TOK, MAIN),
            ram(16, 256),
            ram(SEQ, 128),
            ram(256, 128),
            ram(2 * PAD, PAD),
            ram(4, 2048, 512),
            ram(RING, PAD, 256),
            ram(2, RING, TOK, MAIN),
            ram(RING, 32, 256),
            ram(2, RING, SEQ, 256),
            ram(RING, 2, 2, 16, 128),
            ram(2, 2, PAD, MAIN),
            ram(2, 32, PAD),
            ram(2, PAD, 32),
            *ring((2,), PAD, TOK),
            ram(PAD, TOK),
            ram(PAD, TOK),
            ram(2, PAD, TOK),
            ram(RING, 2, 2, 16, PAD),
            *ring((2,), PAD, 128),
            ram(PAD, 128),
            ram(PAD, 128),
            ram(PAD, 2048),
            ram(RING, PAD, 256),
            ram(RING, PAD, 256),
            *ring((2,), PAD, 128),
            ram(PAD, 128),
            ram(PAD, 128),
            ram(PAD, 128),
            ram(PAD, 128),
            dma((N_SEM,)),
            dma((N_SEM,)),
            dma((RING,)),
            dma((RING,)),
            dma((6,)),
            pltpu.VMEM((RING, 2 * PAD, TOK), f32),
            pltpu.VMEM((RING, PAD, 256), f32),
        ],
        compiler_params=pltpu.CompilerParams(
            collective_id=0, has_side_effects=True, vmem_limit_bytes=56 * 2**20
        ),
    )(out_grads, layer_inputs, query_grads, query_inputs, basis_out, basis_in)


def solution(mesh):
    in_specs = (
        P("dp", "panel"),
        P("dp", None),
        P("dp", "panel"),
        P("dp", None),
        P("panel", "dp"),
        P(None, "panel"),
    )
    out_specs = (P("dp", "panel"), P("dp", "panel"))
    return jax.shard_map(
        per_device, mesh=mesh, in_specs=in_specs, out_specs=out_specs, check_vma=False
    )
```
